32 devices in a mesh: row: 4 (over z), col: 8 (over y, x, core).
Axes of the slice: x: 2, y: 2, z: 4, core: 2. Of those that a mesh axis runs over, the one named last changes fastest.
Arguments:
- psi_val: float32 [64, 128, 128, 128], P(None, 'row', 'col'), may hold values from -6 to 6
- psi_cond: float32 [64, 128, 128, 128], P(None, 'row', 'col'), may hold values from -6 to 6
- eps_val: float32 [64], replicated, may hold values from -12 to -1
- eps_cond: float32 [64], replicated, may hold values from 1 to 12
- val_index: int32 [32], replicated, may hold values from 0 to 63
- cond_index: int32 [32], replicated, may hold values from 0 to 63
- gmap: int32 [8192], replicated, may hold values from 0 to 2097151, as said below
- chi0_in: float32 [2, 8192, 8192], P(None, 'row', 'col'), may hold values from -6 to 6
Outputs:
- chi0_out: float32 [2, 8192, 8192], P(None, 'row', 'col')
The draws below stay inside these ranges and needn't reach their ends.
Inputs may be any that keep to these rules, and one draw needn't show every extreme that they name: gmap holds 8192 distinct entries. Entries g of device block d = g // 256 (d = r * 8 + c) have ky in [r * 32, (r + 1) * 32) and kz in [c * 16, (c + 1) * 16); kx is any.
All inputs are finite; a program needn't handle non-finite values.
Results may differ from the reference program's by a relative error of at most 0.000068.
Values sent between devices are 32-bit elements; how exact they have to be, the bound alone decides.
A program may use at most 256 MiB of HBM per device.

```python
import math
import jax
import jax.numpy as jnp
from jax import lax

GRID = 128
NG = 8192
NV = 64
NC = 64
P_SIZE = 32
RB = 32
CB = 16
GDEV = 256
MESH_ROWS = 4
MESH_COLS = 8


def pick_block(key, target, block):
    perm = jax.random.permutation(key, block).astype(jnp.int32)
    where_at = jnp.argmax(perm == target)
    first = perm[0]
    perm = perm.at[where_at].set(first)
    perm = perm.at[0].set(target)
    return perm[:GDEV]


def draw_gmap(key, part):
    block = RB * CB * GRID
    count = MESH_ROWS * MESH_COLS
    keys = jax.random.split(key, count)
    device_ids = jnp.arange(count, dtype=jnp.int32)
    targets = jnp.where(device_ids == count - 1, block - 1, 0).astype(jnp.int32)
    picks = jax.vmap(lambda k, t: pick_block(k, t, block))(keys, targets).astype(jnp.int32)
    device = device_ids[:, None]
    row_pos = device // MESH_COLS
    col_pos = device % MESH_COLS
    freq_x = picks % GRID
    rest = picks // GRID
    freq_z = col_pos * CB + rest % CB
    freq_y = row_pos * RB + rest // CB
    return ((freq_x * GRID + freq_y) * GRID + freq_z).reshape(-1).astype(jnp.int32)


def place_ends(entries, rng, smallest, top_value):
    dims = entries.shape
    spot = [jax.random.randint(jax.random.fold_in(rng, axis), (), 0, dims[axis]) for axis in range(len(dims))]
    entries = entries.at[tuple(spot)].set(smallest)
    longest = dims.index(max(dims))
    spot[longest] = (spot[longest] + 1) % dims[longest]
    return entries.at[tuple(spot)].set(top_value)


def levels(stream_key, shape, pieces, smallest, top_value):
    def one(dim, blocks):
        steps = jax.random.uniform(jax.random.fold_in(jax.random.fold_in(stream_key, 6), dim), (blocks,), jnp.float32, smallest / len(pieces), top_value / len(pieces))
        return jnp.repeat(jnp.exp(steps), shape[dim] // blocks).reshape((-1,) + (1,) * (len(shape) - dim - 1))

    loudness = one(*pieces[0])
    for cut in pieces[1:]:
        loudness = loudness * one(*cut)
    return loudness


def scatter_about(key, shape, deviation, most, cuts=(), kind=jnp.bfloat16):
    drawn = jax.random.normal(key, shape, jnp.float32) * deviation
    if len(cuts) > 0:
        drawn = levels(key, shape, cuts, -0.22, 0.18) * drawn
    return jnp.clip(drawn, min=-most, max=most).astype(kind)


def setup_inputs(seed: int = 0) -> dict:
    key_list = jax.random.split(jax.random.key(seed), 9)
    return {
        "psi_val": scatter_about(key_list[0], (NV, GRID, GRID, GRID), 1.0, 6.0, ((1, 4), (2, 8)), jnp.float32),
        "psi_cond": scatter_about(key_list[1], (NC, GRID, GRID, GRID), 1.0, 6.0, ((1, 4), (2, 8)), jnp.float32),
        "eps_val": jnp.clip(jax.random.uniform(key_list[2], (NV,), jnp.float32, -12.0, -1.0), -12.0, -1.0),
        "eps_cond": jnp.clip(jax.random.uniform(key_list[3], (NC,), jnp.float32, 1.0, 12.0), 1.0, 12.0),
        "val_index": place_ends(jax.random.randint(key_list[4], (P_SIZE,), 0, NV), jax.random.fold_in(key_list[4], 1), 0, NV - 1).astype(jnp.int32),
        "cond_index": place_ends(jax.random.randint(key_list[5], (P_SIZE,), 0, NC), jax.random.fold_in(key_list[5], 1), 0, NC - 1).astype(jnp.int32),
        "gmap": draw_gmap(jax.random.fold_in(key_list[8], 71), 0),
        "chi0_in": scatter_about(key_list[7], (2, NG, NG), 1.0, 6.0, ((1, 4), (2, 8)), jnp.float32),
    }


def contract_pairs(left, right):
    return lax.dot_general(left, right, (((0,), (0,)), ((), ())), precision=lax.Precision.HIGHEST, preferred_element_type=jnp.float32)

def reference(psi_val, psi_cond, eps_val, eps_cond, val_index, cond_index, gmap, chi0_in):
    scale = 1.0 / math.sqrt(GRID ** 3)

    def one_pair(pair):
        vband, cband = pair
        rho = psi_val[vband] * psi_cond[cband]
        spec = jnp.fft.fftn(rho).reshape(-1)[gmap]
        return (jnp.real(spec).astype(jnp.float32) * scale, jnp.imag(spec).astype(jnp.float32) * scale)
    m_re, m_im = lax.map(one_pair, (val_index, cond_index))
    weight = -6.0 / (math.sqrt(P_SIZE) * (eps_cond[cond_index] - eps_val[val_index]))
    weight = weight[:, None]
    out_re = chi0_in[0] + contract_pairs(weight * m_re, m_re) + contract_pairs(weight * m_im, m_im)
    out_im = chi0_in[1] + contract_pairs(weight * m_im, m_re) - contract_pairs(weight * m_re, m_im)
    return jnp.stack([out_re, out_im])
```

```python
import functools
import math

import jax
import jax.numpy as jnp
import ml_dtypes
import numpy as np
from jax import lax
from jax.experimental import pallas as pl
from jax.experimental.pallas import tpu as pltpu
from jax.sharding import PartitionSpec as P

F32 = jnp.float32
BF16 = jnp.bfloat16
LANES = 128
ROW_PAD = 72
VMEM_BYTES = 60 * 1024 * 1024
NT = (((1,), (1,)), ((), ()))


def split(value):
    high = value.astype(BF16)
    return high, (value - high.astype(F32)).astype(BF16)


def z_tables(grid):
    half = grid // 2 + 1
    freq = np.arange(half)[:, None] * np.arange(grid)[None, :] % grid
    angle = freq * (2.0 * math.pi / grid)
    scale = 1.0 / math.sqrt(grid**3)
    table = np.zeros((2 * ROW_PAD, grid), np.float32)
    table[:half] = np.cos(angle) * scale
    table[ROW_PAD : ROW_PAD + half] = -np.sin(angle) * scale
    high = table.astype(ml_dtypes.bfloat16)
    low = (table - high.astype(np.float32)).astype(ml_dtypes.bfloat16)
    return jnp.asarray(np.concatenate([high, high], axis=1)), jnp.asarray(low)


def sort_points(gmap, grid):
    count = gmap.shape[0]
    blocks = count // LANES
    kx = gmap // (grid * grid)
    ky = gmap // grid % grid
    kz = gmap % grid
    flip = kz > grid // 2
    fold = jnp.where(flip, grid - kz, kz)
    kx = jnp.where(flip, (grid - kx) % grid, kx)
    ky = jnp.where(flip, (grid - ky) % grid, ky)
    sign = jnp.where(flip, -1.0, 1.0).astype(F32)
    bins = jnp.arange(LANES, dtype=jnp.int32)
    hot = (fold.reshape(blocks, LANES)[:, :, None] == bins).astype(BF16)
    before = (bins[:, None] > bins[None, :]).astype(BF16)
    within = jnp.einsum("ab,jbk->jak", before, hot, preferred_element_type=F32)
    totals = jnp.sum(hot.astype(F32), axis=1).astype(BF16)
    offset = jnp.dot(before[:blocks, :blocks], totals, preferred_element_type=F32)
    start = jnp.sum(jnp.dot(totals, before.T, preferred_element_type=F32), axis=0)
    place = jnp.sum(hot.astype(F32) * (within + offset[:, None, :] + start), axis=2)
    place = place.reshape(-1).astype(jnp.int32)
    major = (place[:, None] // LANES == jnp.arange(blocks, dtype=jnp.int32)).astype(F32)
    minor = (place[:, None] % LANES == bins).astype(BF16)
    values = jnp.stack([kx.astype(F32), ky.astype(F32), fold.astype(F32), sign], axis=1)
    spread = (values[:, :, None] * major[:, None, :]).reshape(count, 4 * blocks).astype(BF16)
    ordered = lax.dot_general(spread, minor, (((0,), (0,)), ((), ())), preferred_element_type=F32)
    return place, ordered


def partial_kernel(
    dims, val_ref, cond_ref, first_ref, last_ref, corner_ref,
    ordered_ref, wide_ref, low_ref, cos_ref, psi_val_ref, psi_cond_ref,
    out_ref, val_buf, cond_buf, z_buf, zz_buf, acc_ref, sems,
):
    pairs, xb, yb, grid, chunks = dims
    rows = xb * yb
    xi_count = 64 // yb
    xo_count = xb // xi_count
    width = xo_count * pairs
    half = grid // 2 + 1

    def copies(p):
        spot = pl.ds(p * rows, rows)
        return (
            pltpu.make_async_copy(psi_val_ref.at[val_ref[p]], val_buf.at[spot], sems.at[0, p]),
            pltpu.make_async_copy(psi_cond_ref.at[cond_ref[p]], cond_buf.at[spot], sems.at[1, p]),
        )

    @pl.loop(0, pairs)
    def _(p):
        for copy in copies(p):
            copy.start()

    @pl.loop(0, pairs)
    def _(p):
        for copy in copies(p):
            copy.wait()

    @pl.loop(0, 64)
    def _(u):
        y, xi = u // xi_count, u % xi_count
        parts = []
        for xo in range(xo_count):
            spot = pl.ds((xo * xi_count + xi) * yb + y, pairs, stride=rows)
            parts.append(val_buf[spot, :] * cond_buf[spot, :])
        rho = jnp.concatenate(parts, axis=0)
        high, low = split(rho)
        both = jnp.concatenate([high, low], axis=1)
        z = lax.dot_general(wide_ref[...], both, NT, preferred_element_type=F32)
        z = z + lax.dot_general(low_ref[...], high, NT, preferred_element_type=F32)
        for t in range(width // LANES):
            lanes = slice(t * LANES, (t + 1) * LANES)
            z_buf[t, pl.ds(u, ROW_PAD, stride=LANES), :] = z[:ROW_PAD, lanes]
            z_buf[t, pl.ds(64 + u, ROW_PAD, stride=LANES), :] = z[ROW_PAD:, lanes]

    @pl.loop(0, half)
    def _(kz):
        for t in range(width // LANES):
            high, low = split(z_buf[t, pl.ds(pl.multiple_of(kz * LANES, LANES), LANES), :])
            lanes = slice(t * LANES, (t + 1) * LANES)
            zz_buf[pl.ds(pl.multiple_of(kz * 256, 256), LANES), lanes] = high
            zz_buf[pl.ds(pl.multiple_of(kz * 256 + LANES, LANES), LANES), lanes] = low

    lane = lax.broadcasted_iota(jnp.int32, (LANES, LANES), 1)
    u_lane = lane % 64
    y_lane, xi_lane = u_lane // xi_count, u_lane % xi_count
    is_im = lane >= 64
    table = jnp.broadcast_to(cos_ref[...], (LANES, LANES))
    quarter = grid // 4

    def cosine(steps):
        return jnp.take_along_axis(table, steps & (grid - 1), axis=1, mode="promise_in_bounds")

    @pl.loop(0, chunks)
    def _(j):
        def column(v):
            row = ordered_ref[pl.ds(v * chunks + j, 1), :]
            return jnp.broadcast_to(row, (LANES, LANES)).T

        kx = column(0).astype(jnp.int32)
        ky = column(1).astype(jnp.int32)
        fold = column(2)
        sign = column(3)
        steps = ky * y_lane + kx * xi_lane
        top = cosine(steps - jnp.where(is_im, quarter, 0))
        bottom = cosine(steps + jnp.where(is_im, 0, quarter))
        high, low = split(jnp.concatenate([top, bottom], axis=0))
        both = jnp.concatenate([high, high], axis=1)
        acc_ref[...] = jnp.zeros_like(acc_ref)

        @pl.loop(first_ref[j], last_ref[j] + 1)
        def _(f):
            base = pl.multiple_of(f * 256, 256)
            result = jnp.dot(both, zz_buf[pl.ds(base, 256), :], preferred_element_type=F32)
            result = result + jnp.dot(low, zz_buf[pl.ds(base, LANES), :], preferred_element_type=F32)
            mine = fold == f.astype(F32)
            for t in range(width // LANES):
                lanes = slice(t * LANES, (t + 1) * LANES)
                for s in range(2):
                    spot = slice(s * LANES, (s + 1) * LANES)
                    acc_ref[spot, lanes] = jnp.where(mine, result[spot, lanes], acc_ref[spot, lanes])

        m_re = jnp.zeros((LANES, LANES), F32)
        m_im = jnp.zeros((LANES, LANES), F32)
        for t in range(width // LANES):
            lanes = slice(t * LANES, (t + 1) * LANES)
            x_lane = corner_ref[0] + (t * LANES + lane) // pairs * xi_count
            steps = kx * x_lane + ky * corner_ref[1]
            cos_p, sin_p = cosine(steps), cosine(steps - quarter)
            a_re, a_im = acc_ref[:LANES, lanes], acc_ref[LANES:, lanes]
            m_re = m_re + a_re * cos_p + a_im * sin_p
            m_im = m_im + a_im * cos_p - a_re * sin_p
        shift = LANES // 2
        while shift >= pairs:
            m_re = m_re + pltpu.roll(m_re, shift, 1)
            m_im = m_im + pltpu.roll(m_im, shift, 1)
            shift //= 2
        m_im = m_im * sign
        spot = pl.ds(pl.multiple_of(j * LANES, LANES), LANES)
        if pairs < LANES:
            group = chunks * 2 * pairs // LANES
            spot = pl.ds(pl.multiple_of(j % group * LANES, LANES), LANES)
            both_parts = jnp.where(lane // pairs % 2 == 0, m_re, m_im)
            out_ref[spot, :] = jnp.where(lane // (2 * pairs) == j // group, both_parts, out_ref[spot, :])
        else:
            out_ref[spot, :LANES] = m_re
            out_ref[spot, LANES:] = m_im


def sum_plan(rows, mesh_rows, mesh_cols):
    col_bits = [("col", b) for b in range(mesh_cols.bit_length() - 1)]
    row_bits = [("row", b) for b in range(mesh_rows.bit_length() - 1)]
    orders = (
        col_bits + row_bits,
        col_bits[:1] + col_bits[:0:-1] + row_bits,
        col_bits[:1] + row_bits + col_bits[1:],
    )
    unit = 8 * mesh_rows * mesh_cols
    units = rows // unit
    first = -(-units * 3 // 8)
    counts = (first, first, units - 2 * first)
    parts, base = [], 0
    for order, count in zip(orders, counts):
        if count:
            parts.append((base, count * unit, count, order))
            base += count * unit
    return parts


def all_sum_kernel(parts, steps, in_ref, out_ref, data, land, send_sems, recv_sems):
    def bit_of(axis, bit):
        return lax.axis_index(axis) // 2**bit % 2

    def partner(axis, bit):
        return {axis: lax.axis_index(axis) + (1 - 2 * bit_of(axis, bit)) * 2**bit}

    barrier = pltpu.get_barrier_semaphore()
    for axis, bit in parts[0][3]:
        pl.semaphore_signal(barrier, inc=1, device_id=partner(axis, bit), device_id_type=pl.DeviceIdType.MESH)
    pl.semaphore_wait(barrier, steps)

    layout = []
    for base, rows, _, order in parts:
        here, size, spots, lands = base, rows, [], base
        for axis, bit in order:
            size //= 2
            side = bit_of(axis, bit)
            keep = pl.multiple_of(here + side * size, 8)
            away = pl.multiple_of(here + (1 - side) * size, 8)
            spots.append((keep, away, size, lands))
            lands += size
            here = keep
        layout.append(spots)

    def copy_of(k, step):
        order = parts[k][3]
        if step < steps:
            keep, away, size, lands = layout[k][step]
            source = (in_ref if step == 0 else data).at[pl.ds(away, size)]
            target = land.at[pl.ds(lands, size)]
            axis, bit = order[step]
        else:
            back = 2 * steps - 1 - step
            keep, away, size, lands = layout[k][back]
            source = target = out_ref.at[pl.ds(keep, size)]
            axis, bit = order[back]
        return pltpu.make_async_remote_copy(
            src_ref=source,
            dst_ref=target,
            send_sem=send_sems.at[k, step],
            recv_sem=recv_sems.at[k, step],
            device_id=partner(axis, bit),
            device_id_type=pl.DeviceIdType.MESH,
        )

    def add(k, step):
        keep, _, size, lands = layout[k][step]
        source = in_ref if step == 0 else data
        target = out_ref if step == steps - 1 else data
        piece = 8 * parts[k][2] * 2 ** min(steps - step - 1, 2)

        @pl.loop(0, size // piece)
        def _(i):
            spot = pl.ds(pl.multiple_of(keep + i * piece, 8), piece)
            target[spot, :] = source[spot, :] + land[pl.ds(pl.multiple_of(lands + i * piece, 8), piece), :]

    for k in range(len(parts)):
        copy_of(k, 0).start()
    for step in range(2 * steps):
        for k in range(len(parts)):
            copy_of(k, step).wait_recv()
            if step < steps:
                add(k, step)
            if step < 2 * steps - 1:
                copy_of(k, step + 1).start()
    for step in range(2 * steps):
        for k in range(len(parts)):
            copy_of(k, step).wait_send()


def all_sum(value, mesh_rows, mesh_cols):
    parts = sum_plan(value.shape[0], mesh_rows, mesh_cols)
    steps = len(parts[0][3])
    vmem_spec = pl.BlockSpec(memory_space=pltpu.VMEM)
    return pl.pallas_call(
        functools.partial(all_sum_kernel, parts, steps),
        out_shape=jax.ShapeDtypeStruct(value.shape, F32),
        in_specs=[vmem_spec],
        out_specs=vmem_spec,
        scratch_shapes=[
            pltpu.VMEM(value.shape, F32),
            pltpu.VMEM(value.shape, F32),
            pltpu.SemaphoreType.DMA((len(parts), 2 * steps)),
            pltpu.SemaphoreType.DMA((len(parts), 2 * steps)),
        ],
        compiler_params=pltpu.CompilerParams(
            collective_id=0, has_side_effects=True, vmem_limit_bytes=VMEM_BYTES
        ),
        name="all_sum",
    )(value)


def update_kernel(dims, row_place, col_place, total_ref, weight_ref, chi_ref, out_ref, m_ref, row_buf, col_buf, right_buf):
    pairs, step_rows, cols, wide = dims
    step = pl.program_id(0)

    def gather(place, base, buf, count):
        @pl.loop(0, count // 8)
        def _(i):
            for k in range(8):
                buf[pl.ds(i * 8 + k, 1), :] = m_ref[pl.ds(place[base + i * 8 + k], 1), :]

    def join(value, right):
        high, low = split(value)
        if 2 * pairs < LANES:
            lane = lax.broadcasted_iota(jnp.int32, value.shape, 1)
            keep = lane < 2 * pairs
            high32, low32 = high.astype(F32), low.astype(F32)
            if right:
                return jnp.concatenate([high, jnp.where(keep, low32, 0.0).astype(BF16)], axis=1)
            return jnp.concatenate(
                [jnp.where(keep, high32, low32).astype(BF16), jnp.where(keep, high32, 0.0).astype(BF16)], axis=1
            )
        return jnp.concatenate([high, high, low] if right else [high, low, high], axis=1)

    @pl.when(step == 0)
    def _():
        packed = total_ref.shape[0]
        piece = 64

        @pl.loop(0, packed // piece)
        def _(i):
            value = total_ref[pl.ds(pl.multiple_of(i * piece, piece), piece), :]
            lane = lax.broadcasted_iota(jnp.int32, value.shape, 1)
            for q in range(m_ref.shape[0] // packed):
                part = value
                if 2 * pairs < wide:
                    part = jnp.where(lane // (2 * pairs) == q, value, 0.0)
                    shift = 2 * pairs
                    while shift < wide:
                        part = part + pltpu.roll(part, shift, 1)
                        shift *= 2
                m_ref[pl.ds(pl.multiple_of(q * packed + i * piece, piece), piece), :] = part

        gather(col_place, 0, col_buf, cols)
        right_buf[...] = join(col_buf[...], True)

    gather(row_place, step * step_rows, row_buf, step_rows)
    left = row_buf[...] * weight_ref[...]
    lane = lax.broadcasted_iota(jnp.int32, left.shape, 1)
    turned = pltpu.roll(left, wide - pairs, 1)
    turned = jnp.where(lane // pairs % 2 == 0, turned, -turned)
    out_ref[0] = chi_ref[0] + lax.dot_general(join(left, False), right_buf[...], NT, preferred_element_type=F32)
    out_ref[1] = chi_ref[1] + lax.dot_general(join(turned, False), right_buf[...], NT, preferred_element_type=F32)


def on_device(psi_val, psi_cond, eps_val, eps_cond, val_index, cond_index, gmap, chi0_in):
    pairs = val_index.shape[0]
    bands_v, xb, yb, grid = psi_val.shape
    bands_c = psi_cond.shape[0]
    points = gmap.shape[0]
    chunks = points // LANES
    row_pos, col_pos = lax.axis_index("row"), lax.axis_index("col")
    place, ordered = sort_points(gmap, grid)
    fold = ordered[2 * chunks : 3 * chunks].astype(jnp.int32)
    corner = jnp.stack([row_pos * xb, col_pos * yb]).astype(jnp.int32)
    z_wide, z_low = z_tables(grid)
    cos_row = jnp.asarray(np.cos(np.arange(grid) * (2.0 * math.pi / grid))[None, :], F32)
    wide = max(LANES, 2 * pairs)
    xi_count = 64 // yb
    width = xb // xi_count * pairs
    rows = xb * yb
    any_spec = pl.BlockSpec(memory_space=pl.ANY)
    vmem_spec = pl.BlockSpec(memory_space=pltpu.VMEM)
    partial = pl.pallas_call(
        functools.partial(partial_kernel, (pairs, xb, yb, grid, chunks)),
        out_shape=jax.ShapeDtypeStruct((points * 2 * pairs // wide, wide), F32),
        grid_spec=pltpu.PrefetchScalarGridSpec(
            num_scalar_prefetch=5,
            grid=(),
            in_specs=[vmem_spec] * 4 + [any_spec] * 2,
            out_specs=vmem_spec,
            scratch_shapes=[
                pltpu.VMEM((pairs * rows, grid), F32),
                pltpu.VMEM((pairs * rows, grid), F32),
                pltpu.VMEM((width // LANES, ROW_PAD * LANES, LANES), F32),
                pltpu.VMEM(((grid // 2 + 1) * 256, width), BF16),
                pltpu.VMEM((256, width), F32),
                pltpu.SemaphoreType.DMA((2, pairs)),
            ],
        ),
        compiler_params=pltpu.CompilerParams(vmem_limit_bytes=VMEM_BYTES),
        name="partial_elements",
    )(
        val_index, cond_index, fold[:, 0], fold[:, LANES - 1], corner,
        ordered, z_wide, z_low, cos_row,
        psi_val.reshape(bands_v, rows, grid), psi_cond.reshape(bands_c, rows, grid),
    )
    total = all_sum(partial, lax.axis_size("row"), lax.axis_size("col"))

    val_hot = val_index[:, None] == jnp.arange(bands_v, dtype=jnp.int32)[None, :]
    cond_hot = cond_index[:, None] == jnp.arange(bands_c, dtype=jnp.int32)[None, :]
    energy_v = jnp.sum(jnp.where(val_hot, eps_val[None, :], 0.0), axis=1)
    energy_c = jnp.sum(jnp.where(cond_hot, eps_cond[None, :], 0.0), axis=1)
    weight = -6.0 / (math.sqrt(pairs) * (energy_c - energy_v))
    weight = jnp.tile(weight, wide // pairs)[None, :]

    _, row_span, col_span = chi0_in.shape
    row_place = lax.dynamic_slice_in_dim(place, row_pos * row_span, row_span, 0)
    col_place = lax.dynamic_slice_in_dim(place, col_pos * col_span, col_span, 0)
    step_rows = 256
    k_width = 256 if 2 * pairs < LANES else 3 * wide
    chi_spec = pl.BlockSpec((2, step_rows, col_span), lambda i, *_: (0, i, 0))
    return pl.pallas_call(
        functools.partial(update_kernel, (pairs, step_rows, col_span, wide)),
        out_shape=jax.ShapeDtypeStruct(chi0_in.shape, F32),
        grid_spec=pltpu.PrefetchScalarGridSpec(
            num_scalar_prefetch=2,
            grid=(row_span // step_rows,),
            in_specs=[vmem_spec, vmem_spec, chi_spec],
            out_specs=chi_spec,
            scratch_shapes=[
                pltpu.VMEM((points, wide), F32),
                pltpu.VMEM((step_rows, wide), F32),
                pltpu.VMEM((col_span, wide), F32),
                pltpu.VMEM((col_span, k_width), BF16),
            ],
        ),
        compiler_params=pltpu.CompilerParams(vmem_limit_bytes=VMEM_BYTES),
        name="chi_update",
    )(row_place, col_place, total, weight, chi0_in)


def solution(mesh):
    return jax.shard_map(
        on_device,
        mesh=mesh,
        in_specs=(
            P(None, "row", "col", None),
            P(None, "row", "col", None),
            P(),
            P(),
            P(),
            P(),
            P(),
            P(None, "row", "col"),
        ),
        out_specs=P(None, "row", "col"),
        check_vma=False,
    )
```

```python
import functools
import math

import jax
import jax.numpy as jnp
import ml_dtypes
import numpy as np
from jax import lax
from jax.experimental import pallas as pl
from jax.experimental.pallas import tpu as pltpu
from jax.sharding import PartitionSpec as P

F32 = jnp.float32
BF16 = jnp.bfloat16
LANES = 128
ROW_PAD = 72
VMEM_BYTES = 60 * 1024 * 1024
NT = (((1,), (1,)), ((), ()))


def split(value):
    high = value.astype(BF16)
    return high, (value - high.astype(F32)).astype(BF16)


def z_tables(grid):
    half = grid // 2 + 1
    freq = np.arange(half)[:, None] * np.arange(grid)[None, :] % grid
    angle = freq * (2.0 * math.pi / grid)
    scale = 1.0 / math.sqrt(grid**3)
    table = np.zeros((2 * ROW_PAD, grid), np.float32)
    table[:half] = np.cos(angle) * scale
    table[ROW_PAD : ROW_PAD + half] = -np.sin(angle) * scale
    high = table.astype(ml_dtypes.bfloat16)
    low = (table - high.astype(np.float32)).astype(ml_dtypes.bfloat16)
    top = np.concatenate([high, high], axis=1)
    return jnp.asarray(np.concatenate([top, np.concatenate([low, np.zeros_like(low)], axis=1)], axis=0))


def sort_points(gmap, grid):
    count = gmap.shape[0]
    blocks = count // LANES
    kx = gmap // (grid * grid)
    ky = gmap // grid % grid
    kz = gmap % grid
    flip = kz > grid // 2
    fold = jnp.where(flip, grid - kz, kz)
    kx = jnp.where(flip, (grid - kx) % grid, kx)
    ky = jnp.where(flip, (grid - ky) % grid, ky)
    sign = jnp.where(flip, -1.0, 1.0).astype(F32)
    bins = jnp.arange(LANES, dtype=jnp.int32)
    hot = (fold.reshape(blocks, LANES)[:, :, None] == bins).astype(BF16)
    before = (bins[:, None] > bins[None, :]).astype(BF16)
    within = jnp.einsum("ab,jbk->jak", before, hot, preferred_element_type=F32)
    totals = jnp.sum(hot.astype(F32), axis=1).astype(BF16)
    offset = jnp.dot(before[:blocks, :blocks], totals, preferred_element_type=F32)
    start = jnp.sum(jnp.dot(totals, before.T, preferred_element_type=F32), axis=0)
    place = jnp.sum(hot.astype(F32) * (within + offset[:, None, :] + start), axis=2)
    place = place.reshape(-1).astype(jnp.int32)
    major = (place[:, None] // LANES == jnp.arange(blocks, dtype=jnp.int32)).astype(F32)
    minor = (place[:, None] % LANES == bins).astype(BF16)
    values = jnp.stack([kx.astype(F32), ky.astype(F32), fold.astype(F32), sign], axis=1)
    spread = (values[:, :, None] * major[:, None, :]).reshape(count, 4 * blocks).astype(BF16)
    ordered = lax.dot_general(spread, minor, (((0,), (0,)), ((), ())), preferred_element_type=F32)
    return place, ordered


def partial_kernel(
    dims, val_ref, cond_ref, first_ref, last_ref, corner_ref,
    ordered_ref, wide_ref, cos_ref, psi_val_ref, psi_cond_ref,
    out_ref, val_buf, cond_buf, z_buf, zz_buf, sems,
):
    pairs, xb, yb, grid, chunks = dims
    rows = xb * yb
    xi_count = 64 // yb
    xo_count = xb // xi_count
    width = xo_count * pairs
    half = grid // 2 + 1

    def copies(p):
        spot = pl.ds(p * rows, rows)
        return (
            pltpu.make_async_copy(psi_val_ref.at[val_ref[p]], val_buf.at[spot], sems.at[0, p]),
            pltpu.make_async_copy(psi_cond_ref.at[cond_ref[p]], cond_buf.at[spot], sems.at[1, p]),
        )

    @pl.loop(0, pairs)
    def _(p):
        for copy in copies(p):
            copy.start()

    @pl.loop(0, pairs)
    def _(p):
        for copy in copies(p):
            copy.wait()

    def transform(u):
        y, xi = u // xi_count, u % xi_count
        parts = []
        for xo in range(xo_count):
            spot = pl.ds((xo * xi_count + xi) * yb + y, pairs, stride=rows)
            parts.append(val_buf[spot, :] * cond_buf[spot, :])
        high, low = split(jnp.concatenate(parts, axis=0))
        both = jnp.concatenate([high, low], axis=1)
        z = lax.dot_general(wide_ref[...], both, NT, preferred_element_type=F32)
        return z[: 2 * ROW_PAD] + z[2 * ROW_PAD :]

    @pl.loop(0, 16)
    def _(i):
        results = [transform(i * 4 + k) for k in range(4)]
        for k, z in enumerate(results):
            for t in range(width // LANES):
                lanes = slice(t * LANES, (t + 1) * LANES)
                z_buf[t, pl.ds(i * 4 + k, ROW_PAD, stride=LANES), :] = z[:ROW_PAD, lanes]
                z_buf[t, pl.ds(64 + i * 4 + k, ROW_PAD, stride=LANES), :] = z[ROW_PAD:, lanes]

    @pl.loop(0, half)
    def _(kz):
        for t in range(width // LANES):
            high, low = split(z_buf[t, pl.ds(pl.multiple_of(kz * LANES, LANES), LANES), :])
            lanes = slice(t * LANES, (t + 1) * LANES)
            zz_buf[pl.ds(pl.multiple_of(kz * 256, 256), LANES), lanes] = high
            zz_buf[pl.ds(pl.multiple_of(kz * 256 + LANES, LANES), LANES), lanes] = low

    lane = lax.broadcasted_iota(jnp.int32, (LANES, LANES), 1)
    u_lane = lane % 64
    y_lane, xi_lane = u_lane // xi_count, u_lane % xi_count
    is_im = lane >= 64
    table = jnp.broadcast_to(cos_ref[...], (LANES, LANES))
    quarter = grid // 4

    def cosine(steps):
        return jnp.take_along_axis(table, steps & (grid - 1), axis=1, mode="promise_in_bounds")

    def elements(j, bins):
        def column(v):
            row = ordered_ref[pl.ds(v * chunks + j, 1), :]
            return jnp.broadcast_to(row, (LANES, LANES)).T

        kx = column(0).astype(jnp.int32)
        ky = column(1).astype(jnp.int32)
        fold = column(2)
        sign = column(3)
        steps = ky * y_lane + kx * xi_lane
        top = cosine(steps - jnp.where(is_im, quarter, 0))
        bottom = cosine(steps + jnp.where(is_im, 0, quarter))
        left, right = [], []
        for f in bins:
            mine = fold == f.astype(F32)
            high, low = split(jnp.concatenate([jnp.where(mine, top, 0.0), jnp.where(mine, bottom, 0.0)], axis=0))
            base = pl.multiple_of(jnp.minimum(f, half - 1) * 256, 256)
            left += [high, high, low]
            right += [zz_buf[pl.ds(base, 256), :], zz_buf[pl.ds(base, LANES), :]]
        result = jnp.dot(
            jnp.concatenate(left, axis=1), jnp.concatenate(right, axis=0), preferred_element_type=F32
        )
        m_re = jnp.zeros((LANES, LANES), F32)
        m_im = jnp.zeros((LANES, LANES), F32)
        for t in range(width // LANES):
            lanes = slice(t * LANES, (t + 1) * LANES)
            x_lane = corner_ref[0] + (t * LANES + lane) // pairs * xi_count
            steps = kx * x_lane + ky * corner_ref[1]
            cos_p, sin_p = cosine(steps), cosine(steps - quarter)
            a_re, a_im = result[:LANES, lanes], result[LANES:, lanes]
            m_re = m_re + a_re * cos_p + a_im * sin_p
            m_im = m_im + a_im * cos_p - a_re * sin_p
        shift = LANES // 2
        while shift >= pairs:
            m_re = m_re + pltpu.roll(m_re, shift, 1)
            m_im = m_im + pltpu.roll(m_im, shift, 1)
            shift //= 2
        m_im = m_im * sign
        if pairs < LANES:
            return (jnp.where(lane // pairs % 2 == 0, m_re, m_im),)
        return m_re, m_im

    packs = max(1, LANES // (2 * pairs))
    group = chunks // packs
    together = packs if packs > 1 else 2

    @pl.loop(0, chunks // together)
    def _(i):
        numbers = [i + k * (chunks // together) for k in range(together)]
        found = [elements(j, (first_ref[j], first_ref[j] + 1)) for j in numbers]
        if packs > 1:
            value = found[0][0]
            for k in range(1, packs):
                value = jnp.where(lane // (2 * pairs) == k, found[k][0], value)
            out_ref[pl.ds(pl.multiple_of(i * LANES, LANES), LANES), :] = value
        else:
            for j, pieces in zip(numbers, found):
                for t, piece in enumerate(pieces):
                    out_ref[pl.ds(pl.multiple_of(j * LANES, LANES), LANES), t * LANES : (t + 1) * LANES] = piece

    @pl.loop(0, chunks)
    def _(j):
        @pl.loop(first_ref[j] + 2, last_ref[j] + 1)
        def _(f):
            spot = pl.ds(pl.multiple_of(j % group * LANES, LANES), LANES)
            for t, piece in enumerate(elements(j, (f,))):
                if packs > 1:
                    piece = jnp.where(lane // (2 * pairs) == j // group, piece, 0.0)
                lanes = slice(t * LANES, (t + 1) * LANES)
                out_ref[spot, lanes] = out_ref[spot, lanes] + piece


def sum_plan(rows, mesh_rows, mesh_cols):
    col_bits = [("col", b) for b in range(mesh_cols.bit_length() - 1)]
    row_bits = [("row", b) for b in range(mesh_rows.bit_length() - 1)]
    orders = (
        col_bits + row_bits,
        col_bits[:1] + col_bits[:0:-1] + row_bits,
        col_bits[:1] + row_bits + col_bits[1:],
    )
    unit = 8 * mesh_rows * mesh_cols
    units = rows // unit
    first = -(-units * 3 // 8)
    counts = (first, first, units - 2 * first)
    parts, base = [], 0
    for order, count in zip(orders, counts):
        if count:
            parts.append((base, count * unit, count, order))
            base += count * unit
    return parts


def all_sum_kernel(parts, steps, in_ref, out_ref, data, land, send_sems, recv_sems):
    def bit_of(axis, bit):
        return lax.axis_index(axis) // 2**bit % 2

    def partner(axis, bit):
        return {axis: lax.axis_index(axis) + (1 - 2 * bit_of(axis, bit)) * 2**bit}

    barrier = pltpu.get_barrier_semaphore()
    for axis, bit in parts[0][3]:
        pl.semaphore_signal(barrier, inc=1, device_id=partner(axis, bit), device_id_type=pl.DeviceIdType.MESH)
    pl.semaphore_wait(barrier, steps)

    layout = []
    for base, rows, _, order in parts:
        here, size, spots, lands = base, rows, [], base
        for axis, bit in order:
            size //= 2
            side = bit_of(axis, bit)
            keep = pl.multiple_of(here + side * size, 8)
            away = pl.multiple_of(here + (1 - side) * size, 8)
            spots.append((keep, away, size, lands))
            lands += size
            here = keep
        layout.append(spots)

    def copy_of(k, step):
        order = parts[k][3]
        if step < steps:
            keep, away, size, lands = layout[k][step]
            source = (in_ref if step == 0 else data).at[pl.ds(away, size)]
            target = land.at[pl.ds(lands, size)]
            axis, bit = order[step]
        else:
            back = 2 * steps - 1 - step
            keep, away, size, lands = layout[k][back]
            source = target = out_ref.at[pl.ds(keep, size)]
            axis, bit = order[back]
        return pltpu.make_async_remote_copy(
            src_ref=source,
            dst_ref=target,
            send_sem=send_sems.at[k, step],
            recv_sem=recv_sems.at[k, step],
            device_id=partner(axis, bit),
            device_id_type=pl.DeviceIdType.MESH,
        )

    def add(k, step):
        keep, _, size, lands = layout[k][step]
        source = in_ref if step == 0 else data
        target = out_ref if step == steps - 1 else data
        piece = 8 * parts[k][2] * 2 ** min(steps - step - 1, 2)

        @pl.loop(0, size // piece)
        def _(i):
            spot = pl.ds(pl.multiple_of(keep + i * piece, 8), piece)
            target[spot, :] = source[spot, :] + land[pl.ds(pl.multiple_of(lands + i * piece, 8), piece), :]

    for k in range(len(parts)):
        copy_of(k, 0).start()
    for step in range(2 * steps):
        for k in range(len(parts)):
            copy_of(k, step).wait_recv()
            if step < steps:
                add(k, step)
            if step < 2 * steps - 1:
                copy_of(k, step + 1).start()
    for step in range(2 * steps):
        for k in range(len(parts)):
            copy_of(k, step).wait_send()


def all_sum(value, mesh_rows, mesh_cols):
    parts = sum_plan(value.shape[0], mesh_rows, mesh_cols)
    steps = len(parts[0][3])
    vmem_spec = pl.BlockSpec(memory_space=pltpu.VMEM)
    return pl.pallas_call(
        functools.partial(all_sum_kernel, parts, steps),
        out_shape=jax.ShapeDtypeStruct(value.shape, F32),
        in_specs=[vmem_spec],
        out_specs=vmem_spec,
        scratch_shapes=[
            pltpu.VMEM(value.shape, F32),
            pltpu.VMEM(value.shape, F32),
            pltpu.SemaphoreType.DMA((len(parts), 2 * steps)),
            pltpu.SemaphoreType.DMA((len(parts), 2 * steps)),
        ],
        compiler_params=pltpu.CompilerParams(
            collective_id=0, has_side_effects=True, vmem_limit_bytes=VMEM_BYTES
        ),
        name="all_sum",
    )(value)


def update_kernel(dims, row_place, col_place, total_ref, weight_ref, chi_ref, out_ref, m_ref, row_buf, col_buf, right_buf):
    pairs, step_rows, cols, wide = dims
    step = pl.program_id(0)

    def gather(place, base, buf, count):
        @pl.loop(0, count // 16)
        def _(i):
            found = [m_ref[pl.ds(place[base + i * 16 + k], 1), :] for k in range(16)]
            for half in range(2):
                spot = pl.ds(pl.multiple_of(i * 16 + half * 8, 8), 8)
                buf[spot, :] = jnp.concatenate(found[half * 8 : half * 8 + 8], axis=0)

    def join(value):
        high, low = split(value)
        if 2 * pairs < LANES:
            lane = lax.broadcasted_iota(jnp.int32, value.shape, 1)
            keep = lane < 2 * pairs
            high32, low32 = high.astype(F32), low.astype(F32)
            return jnp.concatenate(
                [jnp.where(keep, high32, low32).astype(BF16), jnp.where(keep, high32, 0.0).astype(BF16)], axis=1
            )
        return jnp.concatenate([high, low, high], axis=1)

    def join_right(value):
        high, low = split(value)
        if 2 * pairs < LANES:
            keep = lax.broadcasted_iota(jnp.int32, value.shape, 0) < 2 * pairs
            return jnp.concatenate([high, jnp.where(keep, low.astype(F32), 0.0).astype(BF16)], axis=0)
        return jnp.concatenate([high, high, low], axis=0)

    @pl.when(step == 0)
    def _():
        packed = total_ref.shape[0]
        piece = 64

        @pl.loop(0, packed // piece)
        def _(i):
            value = total_ref[pl.ds(pl.multiple_of(i * piece, piece), piece), :]
            lane = lax.broadcasted_iota(jnp.int32, value.shape, 1)
            for q in range(m_ref.shape[0] // packed):
                part = value
                if 2 * pairs < wide:
                    part = jnp.where(lane // (2 * pairs) == q, value, 0.0)
                    shift = 2 * pairs
                    while shift < wide:
                        part = part + pltpu.roll(part, shift, 1)
                        shift *= 2
                m_ref[pl.ds(pl.multiple_of(q * packed + i * piece, piece), piece), :] = part

        gather(col_place, 0, col_buf, cols)
        right_buf[...] = join_right(col_buf[...].T)

    gather(row_place, step * step_rows, row_buf, step_rows)
    left = row_buf[...] * weight_ref[...]
    lane = lax.broadcasted_iota(jnp.int32, left.shape, 1)
    turned = pltpu.roll(left, wide - pairs, 1)
    turned = jnp.where(lane // pairs % 2 == 0, turned, -turned)
    out_ref[0] = chi_ref[0] + jnp.dot(join(left), right_buf[...], preferred_element_type=F32)
    out_ref[1] = chi_ref[1] + jnp.dot(join(turned), right_buf[...], preferred_element_type=F32)


def on_device(psi_val, psi_cond, eps_val, eps_cond, val_index, cond_index, gmap, chi0_in):
    pairs = val_index.shape[0]
    bands_v, xb, yb, grid = psi_val.shape
    bands_c = psi_cond.shape[0]
    points = gmap.shape[0]
    chunks = points // LANES
    row_pos, col_pos = lax.axis_index("row"), lax.axis_index("col")
    place, ordered = sort_points(gmap, grid)
    fold = ordered[2 * chunks : 3 * chunks].astype(jnp.int32)
    corner = jnp.stack([row_pos * xb, col_pos * yb]).astype(jnp.int32)
    z_wide = z_tables(grid)
    cos_row = jnp.asarray(np.cos(np.arange(grid) * (2.0 * math.pi / grid))[None, :], F32)
    wide = max(LANES, 2 * pairs)
    xi_count = 64 // yb
    width = xb // xi_count * pairs
    rows = xb * yb
    any_spec = pl.BlockSpec(memory_space=pl.ANY)
    vmem_spec = pl.BlockSpec(memory_space=pltpu.VMEM)
    partial = pl.pallas_call(
        functools.partial(partial_kernel, (pairs, xb, yb, grid, chunks)),
        out_shape=jax.ShapeDtypeStruct((points * 2 * pairs // wide, wide), F32),
        grid_spec=pltpu.PrefetchScalarGridSpec(
            num_scalar_prefetch=5,
            grid=(),
            in_specs=[vmem_spec] * 3 + [any_spec] * 2,
            out_specs=vmem_spec,
            scratch_shapes=[
                pltpu.VMEM((pairs * rows, grid), F32),
                pltpu.VMEM((pairs * rows, grid), F32),
                pltpu.VMEM((width // LANES, ROW_PAD * LANES, LANES), F32),
                pltpu.VMEM(((grid // 2 + 1) * 256, width), BF16),
                pltpu.SemaphoreType.DMA((2, pairs)),
            ],
        ),
        compiler_params=pltpu.CompilerParams(vmem_limit_bytes=VMEM_BYTES),
        name="partial_elements",
    )(
        val_index, cond_index, fold[:, 0], fold[:, LANES - 1], corner,
        ordered, z_wide, cos_row,
        psi_val.reshape(bands_v, rows, grid), psi_cond.reshape(bands_c, rows, grid),
    )
    total = all_sum(partial, lax.axis_size("row"), lax.axis_size("col"))

    val_hot = val_index[:, None] == jnp.arange(bands_v, dtype=jnp.int32)[None, :]
    cond_hot = cond_index[:, None] == jnp.arange(bands_c, dtype=jnp.int32)[None, :]
    energy_v = jnp.sum(jnp.where(val_hot, eps_val[None, :], 0.0), axis=1)
    energy_c = jnp.sum(jnp.where(cond_hot, eps_cond[None, :], 0.0), axis=1)
    weight = -6.0 / (math.sqrt(pairs) * (energy_c - energy_v))
    weight = jnp.tile(weight, wide // pairs)[None, :]

    _, row_span, col_span = chi0_in.shape
    row_place = lax.dynamic_slice_in_dim(place, row_pos * row_span, row_span, 0)
    col_place = lax.dynamic_slice_in_dim(place, col_pos * col_span, col_span, 0)
    step_rows = 256
    k_width = 256 if 2 * pairs < LANES else 3 * wide
    chi_spec = pl.BlockSpec((2, step_rows, col_span), lambda i, *_: (0, i, 0))
    return pl.pallas_call(
        functools.partial(update_kernel, (pairs, step_rows, col_span, wide)),
        out_shape=jax.ShapeDtypeStruct(chi0_in.shape, F32),
        grid_spec=pltpu.PrefetchScalarGridSpec(
            num_scalar_prefetch=2,
            grid=(row_span // step_rows,),
            in_specs=[vmem_spec, vmem_spec, chi_spec],
            out_specs=chi_spec,
            scratch_shapes=[
                pltpu.VMEM((points, wide), F32),
                pltpu.VMEM((step_rows, wide), F32),
                pltpu.VMEM((col_span, wide), F32),
                pltpu.VMEM((k_width, col_span), BF16),
            ],
        ),
        compiler_params=pltpu.CompilerParams(vmem_limit_bytes=VMEM_BYTES),
        name="chi_update",
    )(row_place, col_place, total, weight, chi0_in)


def solution(mesh):
    return jax.shard_map(
        on_device,
        mesh=mesh,
        in_specs=(
            P(None, "row", "col", None),
            P(None, "row", "col", None),
            P(),
            P(),
            P(),
            P(),
            P(),
            P(None, "row", "col"),
        ),
        out_specs=P(None, "row", "col"),
        check_vma=False,
    )
```

```python
import functools
import math

import jax
import jax.numpy as jnp
import ml_dtypes
import numpy as np
from jax import lax
from jax.experimental import pallas as pl
from jax.experimental.pallas import tpu as pltpu
from jax.sharding import PartitionSpec as P

F32 = jnp.float32
BF16 = jnp.bfloat16
LANES = 128
ROW_PAD = 72
Z_STRIDE = LANES + 8
VMEM_BYTES = 60 * 1024 * 1024
NT = (((1,), (1,)), ((), ()))


def split(value):
    high = value.astype(BF16)
    return high, (value - high.astype(F32)).astype(BF16)


def z_tables(grid):
    half = grid // 2 + 1
    freq = np.arange(half)[:, None] * np.arange(grid)[None, :] % grid
    angle = freq * (2.0 * math.pi / grid)
    scale = 1.0 / math.sqrt(grid**3)
    table = np.zeros((2 * ROW_PAD, grid), np.float32)
    table[:half] = np.cos(angle) * scale
    table[ROW_PAD : ROW_PAD + half] = -np.sin(angle) * scale
    high = table.astype(ml_dtypes.bfloat16)
    low = (table - high.astype(np.float32)).astype(ml_dtypes.bfloat16)
    top = np.concatenate([high, high], axis=1)
    return jnp.asarray(np.concatenate([top, np.concatenate([low, np.zeros_like(low)], axis=1)], axis=0))


def sort_points(gmap, grid):
    count = gmap.shape[0]
    blocks = count // LANES
    kx = gmap // (grid * grid)
    ky = gmap // grid % grid
    kz = gmap % grid
    flip = kz > grid // 2
    fold = jnp.where(flip, grid - kz, kz)
    kx = jnp.where(flip, (grid - kx) % grid, kx)
    ky = jnp.where(flip, (grid - ky) % grid, ky)
    sign = jnp.where(flip, -1.0, 1.0).astype(F32)
    bins = jnp.arange(LANES, dtype=jnp.int32)
    hot = (fold.reshape(blocks, LANES)[:, :, None] == bins).astype(BF16)
    before = (bins[:, None] > bins[None, :]).astype(BF16)
    within = jnp.einsum("ab,jbk->jak", before, hot, preferred_element_type=F32)
    totals = jnp.sum(hot.astype(F32), axis=1).astype(BF16)
    offset = jnp.dot(before[:blocks, :blocks], totals, preferred_element_type=F32)
    start = jnp.sum(jnp.dot(totals, before.T, preferred_element_type=F32), axis=0)
    place = jnp.sum(hot.astype(F32) * (within + offset[:, None, :] + start), axis=2)
    place = place.reshape(-1).astype(jnp.int32)
    major = (place[:, None] // LANES == jnp.arange(blocks, dtype=jnp.int32)).astype(F32)
    minor = (place[:, None] % LANES == bins).astype(BF16)
    values = jnp.stack([kx.astype(F32), ky.astype(F32), fold.astype(F32), sign], axis=1)
    spread = (values[:, :, None] * major[:, None, :]).reshape(count, 4 * blocks).astype(BF16)
    ordered = lax.dot_general(spread, minor, (((0,), (0,)), ((), ())), preferred_element_type=F32)
    return place, ordered


def partial_kernel(
    dims, val_ref, cond_ref, first_ref, last_ref, corner_ref,
    ordered_ref, wide_ref, cos_ref, psi_val_ref, psi_cond_ref,
    out_ref, val_buf, cond_buf, z_buf, zz_buf, sems,
):
    pairs, xb, yb, grid, chunks = dims
    rows = xb * yb
    xi_count = 64 // yb
    xo_count = xb // xi_count
    width = xo_count * pairs
    half = grid // 2 + 1

    def copies(p):
        spot = pl.ds(pl.multiple_of(p * (rows + 8), 8), rows)
        return (
            pltpu.make_async_copy(psi_val_ref.at[val_ref[p]], val_buf.at[spot], sems.at[0, p]),
            pltpu.make_async_copy(psi_cond_ref.at[cond_ref[p]], cond_buf.at[spot], sems.at[1, p]),
        )

    @pl.loop(0, pairs)
    def _(p):
        for copy in copies(p):
            copy.start()

    @pl.loop(0, pairs)
    def _(p):
        for copy in copies(p):
            copy.wait()

    def transform(u):
        y, xi = u // xi_count, u % xi_count
        parts = []
        for xo in range(xo_count):
            spot = pl.ds((xo * xi_count + xi) * yb + y, pairs, stride=rows + 8)
            parts.append(val_buf[spot, :] * cond_buf[spot, :])
        high, low = split(jnp.concatenate(parts, axis=0))
        both = jnp.concatenate([high, low], axis=1)
        z = lax.dot_general(wide_ref[...], both, NT, preferred_element_type=F32)
        return z[: 2 * ROW_PAD] + z[2 * ROW_PAD :]

    @pl.loop(0, 16)
    def _(i):
        results = [transform(i * 4 + k) for k in range(4)]
        for k, z in enumerate(results):
            for t in range(width // LANES):
                lanes = slice(t * LANES, (t + 1) * LANES)
                z_buf[t, pl.ds(i * 4 + k, ROW_PAD, stride=Z_STRIDE), :] = z[:ROW_PAD, lanes]
                z_buf[t, pl.ds(64 + i * 4 + k, ROW_PAD, stride=Z_STRIDE), :] = z[ROW_PAD:, lanes]

    @pl.loop(0, half)
    def _(kz):
        for t in range(width // LANES):
            high, low = split(z_buf[t, pl.ds(pl.multiple_of(kz * Z_STRIDE, 8), LANES), :])
            lanes = slice(t * LANES, (t + 1) * LANES)
            zz_buf[pl.ds(pl.multiple_of(kz * 256, 256), LANES), lanes] = high
            zz_buf[pl.ds(pl.multiple_of(kz * 256 + LANES, LANES), LANES), lanes] = low

    lane = lax.broadcasted_iota(jnp.int32, (LANES, LANES), 1)
    u_lane = lane % 64
    y_lane, xi_lane = u_lane // xi_count, u_lane % xi_count
    is_im = lane >= 64
    table = jnp.broadcast_to(cos_ref[...], (LANES, LANES))
    quarter = grid // 4

    def cosine(steps):
        return jnp.take_along_axis(table, steps & (grid - 1), axis=1, mode="promise_in_bounds")

    def elements(j, bins):
        def column(v):
            row = ordered_ref[pl.ds(v * chunks + j, 1), :]
            return jnp.broadcast_to(row, (LANES, LANES)).T

        kx = column(0).astype(jnp.int32)
        ky = column(1).astype(jnp.int32)
        fold = column(2)
        sign = column(3)
        steps = ky * y_lane + kx * xi_lane
        top = cosine(steps - jnp.where(is_im, quarter, 0))
        bottom = cosine(steps + jnp.where(is_im, 0, quarter))
        left, right = [], []
        for f in bins:
            mine = fold == f.astype(F32)
            high, low = split(jnp.concatenate([jnp.where(mine, top, 0.0), jnp.where(mine, bottom, 0.0)], axis=0))
            base = pl.multiple_of(jnp.minimum(f, half - 1) * 256, 256)
            left += [high, high, low]
            right += [zz_buf[pl.ds(base, 256), :], zz_buf[pl.ds(base, LANES), :]]
        result = jnp.dot(
            jnp.concatenate(left, axis=1), jnp.concatenate(right, axis=0), preferred_element_type=F32
        )
        m_re = jnp.zeros((LANES, LANES), F32)
        m_im = jnp.zeros((LANES, LANES), F32)
        for t in range(width // LANES):
            lanes = slice(t * LANES, (t + 1) * LANES)
            x_lane = corner_ref[0] + (t * LANES + lane) // pairs * xi_count
            steps = kx * x_lane + ky * corner_ref[1]
            cos_p, sin_p = cosine(steps), cosine(steps - quarter)
            a_re, a_im = result[:LANES, lanes], result[LANES:, lanes]
            m_re = m_re + a_re * cos_p + a_im * sin_p
            m_im = m_im + a_im * cos_p - a_re * sin_p
        shift = LANES // 2
        while shift >= pairs:
            m_re = m_re + pltpu.roll(m_re, shift, 1)
            m_im = m_im + pltpu.roll(m_im, shift, 1)
            shift //= 2
        m_im = m_im * sign
        if pairs < LANES:
            return (jnp.where(lane // pairs % 2 == 0, m_re, m_im),)
        return m_re, m_im

    packs = max(1, LANES // (2 * pairs))
    group = chunks // packs

    @pl.loop(0, group // 2)
    def _(i):
        bases = [i, i + group // 2]
        found = [[elements(b + k * group, (first_ref[b + k * group], first_ref[b + k * group] + 1))
                  for k in range(packs)] for b in bases]
        for b, pieces in zip(bases, found):
            spot = pl.ds(pl.multiple_of(b * LANES, LANES), LANES)
            value = list(pieces[0])
            for k in range(1, packs):
                value[0] = jnp.where(lane // (2 * pairs) == k, pieces[k][0], value[0])
            for t, piece in enumerate(value):
                out_ref[spot, t * LANES : (t + 1) * LANES] = piece

    @pl.loop(0, chunks)
    def _(j):
        @pl.loop(first_ref[j] + 2, last_ref[j] + 1)
        def _(f):
            spot = pl.ds(pl.multiple_of(j % group * LANES, LANES), LANES)
            for t, piece in enumerate(elements(j, (f,))):
                if packs > 1:
                    piece = jnp.where(lane // (2 * pairs) == j // group, piece, 0.0)
                lanes = slice(t * LANES, (t + 1) * LANES)
                out_ref[spot, lanes] = out_ref[spot, lanes] + piece


def sum_plan(rows, mesh_rows, mesh_cols):
    col_bits = [("col", b) for b in range(mesh_cols.bit_length() - 1)]
    row_bits = [("row", b) for b in range(mesh_rows.bit_length() - 1)]
    orders = (
        col_bits + row_bits,
        col_bits[:1] + col_bits[:0:-1] + row_bits,
        col_bits[:1] + row_bits + col_bits[1:],
    )
    unit = 8 * mesh_rows * mesh_cols
    units = rows // unit
    first = -(-units * 3 // 8)
    counts = (first, first, units - 2 * first)
    parts, base = [], 0
    halves = [(o, c - c // 2) for o, c in zip(orders, counts)] + [(o, c // 2) for o, c in zip(orders, counts)]
    for order, count in halves:
        if count:
            parts.append((base, count * unit, count, order))
            base += count * unit
    return parts


def all_sum_kernel(parts, steps, in_ref, out_ref, data, land, send_sems, recv_sems):
    def bit_of(axis, bit):
        return lax.axis_index(axis) // 2**bit % 2

    def partner(axis, bit):
        return {axis: lax.axis_index(axis) + (1 - 2 * bit_of(axis, bit)) * 2**bit}

    barrier = pltpu.get_barrier_semaphore()
    for axis, bit in parts[0][3]:
        pl.semaphore_signal(barrier, inc=1, device_id=partner(axis, bit), device_id_type=pl.DeviceIdType.MESH)
    pl.semaphore_wait(barrier, steps)

    layout = []
    for base, rows, _, order in parts:
        here, size, spots, lands = base, rows, [], base
        for axis, bit in order:
            size //= 2
            side = bit_of(axis, bit)
            keep = pl.multiple_of(here + side * size, 8)
            away = pl.multiple_of(here + (1 - side) * size, 8)
            spots.append((keep, away, size, lands))
            lands += size
            here = keep
        layout.append(spots)

    def copy_of(k, step):
        order = parts[k][3]
        if step < steps:
            keep, away, size, lands = layout[k][step]
            source = (in_ref if step == 0 else data).at[pl.ds(away, size)]
            target = land.at[pl.ds(lands, size)]
            axis, bit = order[step]
        else:
            back = 2 * steps - 1 - step
            keep, away, size, lands = layout[k][back]
            source = target = out_ref.at[pl.ds(keep, size)]
            axis, bit = order[back]
        return pltpu.make_async_remote_copy(
            src_ref=source,
            dst_ref=target,
            send_sem=send_sems.at[k, step],
            recv_sem=recv_sems.at[k, step],
            device_id=partner(axis, bit),
            device_id_type=pl.DeviceIdType.MESH,
        )

    def add(k, step):
        keep, _, size, lands = layout[k][step]
        source = in_ref if step == 0 else data
        target = out_ref if step == steps - 1 else data
        piece = 8 * parts[k][2] * 2 ** min(steps - step - 1, 2)

        @pl.loop(0, size // piece)
        def _(i):
            spot = pl.ds(pl.multiple_of(keep + i * piece, 8), piece)
            target[spot, :] = source[spot, :] + land[pl.ds(pl.multiple_of(lands + i * piece, 8), piece), :]

    for k in range(len(parts)):
        copy_of(k, 0).start()
    for step in range(2 * steps):
        for k in range(len(parts)):
            copy_of(k, step).wait_recv()
            if step < steps:
                add(k, step)
            if step < 2 * steps - 1:
                copy_of(k, step + 1).start()
    for step in range(2 * steps):
        for k in range(len(parts)):
            copy_of(k, step).wait_send()


def all_sum(value, mesh_rows, mesh_cols):
    parts = sum_plan(value.shape[0], mesh_rows, mesh_cols)
    steps = len(parts[0][3])
    vmem_spec = pl.BlockSpec(memory_space=pltpu.VMEM)
    return pl.pallas_call(
        functools.partial(all_sum_kernel, parts, steps),
        out_shape=jax.ShapeDtypeStruct(value.shape, F32),
        in_specs=[vmem_spec],
        out_specs=vmem_spec,
        scratch_shapes=[
            pltpu.VMEM(value.shape, F32),
            pltpu.VMEM(value.shape, F32),
            pltpu.SemaphoreType.DMA((len(parts), 2 * steps)),
            pltpu.SemaphoreType.DMA((len(parts), 2 * steps)),
        ],
        compiler_params=pltpu.CompilerParams(
            collective_id=0, has_side_effects=True, vmem_limit_bytes=VMEM_BYTES
        ),
        name="all_sum",
    )(value)


def update_kernel(
    dims, row_place, col_place, total_ref, weight_ref, chi_ref, out_ref,
    m_ref, row_buf, col_buf, right_buf, chi_buf, sems,
):
    pairs, step_rows, cols, wide = dims
    steps = chi_ref.shape[1] // step_rows

    def arrival(step):
        spot = pl.ds(pl.multiple_of(step * step_rows, step_rows), step_rows)
        return pltpu.make_async_copy(chi_ref.at[:, spot], chi_buf.at[:, spot], sems.at[0, step])

    def departure(step):
        spot = pl.ds(pl.multiple_of(step * step_rows, step_rows), step_rows)
        return pltpu.make_async_copy(chi_buf.at[:, spot], out_ref.at[:, spot], sems.at[1, step])

    @pl.loop(0, steps)
    def _(step):
        arrival(step).start()

    def gather(place, base, buf, count):
        @pl.loop(0, count // 16)
        def _(i):
            found = [m_ref[pl.ds(place[base + i * 16 + k], 1), :] for k in range(16)]
            for half in range(2):
                spot = pl.ds(pl.multiple_of(i * 16 + half * 8, 8), 8)
                buf[spot, :] = jnp.concatenate(found[half * 8 : half * 8 + 8], axis=0)

    def join(value):
        high, low = split(value)
        if 2 * pairs < LANES:
            lane = lax.broadcasted_iota(jnp.int32, value.shape, 1)
            keep = lane < 2 * pairs
            high32, low32 = high.astype(F32), low.astype(F32)
            return jnp.concatenate(
                [jnp.where(keep, high32, low32).astype(BF16), jnp.where(keep, high32, 0.0).astype(BF16)], axis=1
            )
        return jnp.concatenate([high, low, high], axis=1)

    def join_right(value):
        high, low = split(value)
        if 2 * pairs < LANES:
            keep = lax.broadcasted_iota(jnp.int32, value.shape, 0) < 2 * pairs
            return jnp.concatenate([high, jnp.where(keep, low.astype(F32), 0.0).astype(BF16)], axis=0)
        return jnp.concatenate([high, high, low], axis=0)

    packed = total_ref.shape[0]
    piece = 64

    @pl.loop(0, packed // piece)
    def _(i):
        value = total_ref[pl.ds(pl.multiple_of(i * piece, piece), piece), :]
        lane = lax.broadcasted_iota(jnp.int32, value.shape, 1)
        for q in range(m_ref.shape[0] // packed):
            part = value
            if 2 * pairs < wide:
                part = jnp.where(lane // (2 * pairs) == q, value, 0.0)
                shift = 2 * pairs
                while shift < wide:
                    part = part + pltpu.roll(part, shift, 1)
                    shift *= 2
            m_ref[pl.ds(pl.multiple_of(q * packed + i * piece, piece), piece), :] = part

    gather(col_place, 0, col_buf, cols)
    right_buf[...] = join_right(col_buf[...].T)

    @pl.loop(0, steps)
    def _(step):
        gather(row_place, step * step_rows, row_buf, step_rows)
        left = row_buf[...] * weight_ref[...]
        lane = lax.broadcasted_iota(jnp.int32, left.shape, 1)
        turned = pltpu.roll(left, wide - pairs, 1)
        turned = jnp.where(lane // pairs % 2 == 0, turned, -turned)
        arrival(step).wait()
        spot = pl.ds(pl.multiple_of(step * step_rows, step_rows), step_rows)
        for part, factor in enumerate((left, turned)):
            change = jnp.dot(join(factor), right_buf[...], preferred_element_type=F32)
            chi_buf[part, spot, :] = chi_buf[part, spot, :] + change
        departure(step).start()

    @pl.loop(0, steps)
    def _(step):
        departure(step).wait()


def on_device(psi_val, psi_cond, eps_val, eps_cond, val_index, cond_index, gmap, chi0_in):
    pairs = val_index.shape[0]
    bands_v, xb, yb, grid = psi_val.shape
    bands_c = psi_cond.shape[0]
    points = gmap.shape[0]
    chunks = points // LANES
    row_pos, col_pos = lax.axis_index("row"), lax.axis_index("col")
    place, ordered = sort_points(gmap, grid)
    fold = ordered[2 * chunks : 3 * chunks].astype(jnp.int32)
    corner = jnp.stack([row_pos * xb, col_pos * yb]).astype(jnp.int32)
    z_wide = z_tables(grid)
    cos_row = jnp.asarray(np.cos(np.arange(grid) * (2.0 * math.pi / grid))[None, :], F32)
    wide = max(LANES, 2 * pairs)
    xi_count = 64 // yb
    width = xb // xi_count * pairs
    rows = xb * yb
    any_spec = pl.BlockSpec(memory_space=pl.ANY)
    vmem_spec = pl.BlockSpec(memory_space=pltpu.VMEM)
    partial = pl.pallas_call(
        functools.partial(partial_kernel, (pairs, xb, yb, grid, chunks)),
        out_shape=jax.ShapeDtypeStruct((points * 2 * pairs // wide, wide), F32),
        grid_spec=pltpu.PrefetchScalarGridSpec(
            num_scalar_prefetch=5,
            grid=(),
            in_specs=[vmem_spec] * 3 + [any_spec] * 2,
            out_specs=vmem_spec,
            scratch_shapes=[
                pltpu.VMEM((pairs * (rows + 8), grid), F32),
                pltpu.VMEM((pairs * (rows + 8), grid), F32),
                pltpu.VMEM((width // LANES, ROW_PAD * Z_STRIDE, LANES), F32),
                pltpu.VMEM(((grid // 2 + 1) * 256, width), BF16),
                pltpu.SemaphoreType.DMA((2, pairs)),
            ],
        ),
        compiler_params=pltpu.CompilerParams(vmem_limit_bytes=VMEM_BYTES),
        name="partial_elements",
    )(
        val_index, cond_index, fold[:, 0], fold[:, LANES - 1], corner,
        ordered, z_wide, cos_row,
        psi_val.reshape(bands_v, rows, grid), psi_cond.reshape(bands_c, rows, grid),
    )
    total = all_sum(partial, lax.axis_size("row"), lax.axis_size("col"))

    val_hot = val_index[:, None] == jnp.arange(bands_v, dtype=jnp.int32)[None, :]
    cond_hot = cond_index[:, None] == jnp.arange(bands_c, dtype=jnp.int32)[None, :]
    energy_v = jnp.sum(jnp.where(val_hot, eps_val[None, :], 0.0), axis=1)
    energy_c = jnp.sum(jnp.where(cond_hot, eps_cond[None, :], 0.0), axis=1)
    weight = -6.0 / (math.sqrt(pairs) * (energy_c - energy_v))
    weight = jnp.tile(weight, wide // pairs)[None, :]

    _, row_span, col_span = chi0_in.shape
    row_place = lax.dynamic_slice_in_dim(place, row_pos * row_span, row_span, 0)
    col_place = lax.dynamic_slice_in_dim(place, col_pos * col_span, col_span, 0)
    step_rows = 256
    k_width = 256 if 2 * pairs < LANES else 3 * wide
    return pl.pallas_call(
        functools.partial(update_kernel, (pairs, step_rows, col_span, wide)),
        out_shape=jax.ShapeDtypeStruct(chi0_in.shape, F32),
        grid_spec=pltpu.PrefetchScalarGridSpec(
            num_scalar_prefetch=2,
            grid=(),
            in_specs=[vmem_spec, vmem_spec, any_spec],
            out_specs=any_spec,
            scratch_shapes=[
                pltpu.VMEM((points, wide), F32),
                pltpu.VMEM((step_rows, wide), F32),
                pltpu.VMEM((col_span, wide), F32),
                pltpu.VMEM((k_width, col_span), BF16),
                pltpu.VMEM(chi0_in.shape, F32),
                pltpu.SemaphoreType.DMA((2, row_span // step_rows)),
            ],
        ),
        compiler_params=pltpu.CompilerParams(vmem_limit_bytes=VMEM_BYTES),
        name="chi_update",
    )(row_place, col_place, total, weight, chi0_in)


def solution(mesh):
    return jax.shard_map(
        on_device,
        mesh=mesh,
        in_specs=(
            P(None, "row", "col", None),
            P(None, "row", "col", None),
            P(),
            P(),
            P(),
            P(),
            P(),
            P(None, "row", "col"),
        ),
        out_specs=P(None, "row", "col"),
        check_vma=False,
    )
```

```python
import functools
import math

import jax
import jax.numpy as jnp
import ml_dtypes
import numpy as np
from jax import lax
from jax.experimental import pallas as pl
from jax.experimental.pallas import tpu as pltpu
from jax.sharding import PartitionSpec as P

F32 = jnp.float32
BF16 = jnp.bfloat16
LANES = 128
ROW_PAD = 72
Z_STRIDE = LANES + 8
VMEM_BYTES = 60 * 1024 * 1024
NT = (((1,), (1,)), ((), ()))


def split(value):
    high = value.astype(BF16)
    return high, (value - high.astype(F32)).astype(BF16)


def z_tables(grid):
    half = grid // 2 + 1
    freq = np.arange(half)[:, None] * np.arange(grid)[None, :] % grid
    angle = freq * (2.0 * math.pi / grid)
    scale = 1.0 / math.sqrt(grid**3)
    table = np.zeros((2 * ROW_PAD, grid), np.float32)
    table[:half] = np.cos(angle) * scale
    table[ROW_PAD : ROW_PAD + half] = -np.sin(angle) * scale
    high = table.astype(ml_dtypes.bfloat16)
    low = (table - high.astype(np.float32)).astype(ml_dtypes.bfloat16)
    top = np.concatenate([high, high], axis=1)
    return jnp.asarray(np.concatenate([top, np.concatenate([low, np.zeros_like(low)], axis=1)], axis=0))


def sort_points(gmap, grid):
    count = gmap.shape[0]
    blocks = count // LANES
    kx = gmap // (grid * grid)
    ky = gmap // grid % grid
    kz = gmap % grid
    flip = kz > grid // 2
    fold = jnp.where(flip, grid - kz, kz)
    kx = jnp.where(flip, (grid - kx) % grid, kx)
    ky = jnp.where(flip, (grid - ky) % grid, ky)
    sign = flip.astype(F32)
    bins = jnp.arange(LANES, dtype=jnp.int32)
    hot = (fold.reshape(blocks, LANES)[:, :, None] == bins).astype(BF16)
    before = (bins[:, None] > bins[None, :]).astype(BF16)
    within = jnp.einsum("ab,jbk->jak", before, hot, preferred_element_type=F32)
    totals = jnp.sum(hot.astype(F32), axis=1).astype(BF16)
    offset = jnp.dot(before[:blocks, :blocks], totals, preferred_element_type=F32)
    start = jnp.sum(jnp.dot(totals, before.T, preferred_element_type=F32), axis=0)
    place = jnp.sum(hot.astype(F32) * (within + offset[:, None, :] + start), axis=2)
    place = place.reshape(-1).astype(jnp.int32)
    major = (place[:, None] // LANES == jnp.arange(blocks, dtype=jnp.int32)).astype(F32)
    minor = (place[:, None] % LANES == bins).astype(BF16)
    values = jnp.stack([kx.astype(F32), ky.astype(F32), fold.astype(F32), sign], axis=1)
    spread = (values[:, :, None] * major[:, None, :]).reshape(count, 4 * blocks).astype(BF16)
    ordered = lax.dot_general(spread, minor, (((0,), (0,)), ((), ())), preferred_element_type=F32)
    return place, ordered


def partial_kernel(
    dims, val_ref, cond_ref, first_ref, last_ref,
    ordered_ref, wide_ref, cos_ref, psi_val_ref, psi_cond_ref,
    out_ref, val_buf, cond_buf, z_buf, zz_buf, sems,
):
    pairs, xb, yb, grid, chunks = dims
    rows = xb * yb
    xi_count = 64 // yb
    xo_count = xb // xi_count
    width = xo_count * pairs
    half = grid // 2 + 1

    def copies(p):
        spot = pl.ds(pl.multiple_of(p * (rows + 8), 8), rows)
        return (
            pltpu.make_async_copy(psi_val_ref.at[val_ref[p]], val_buf.at[spot], sems.at[0, p]),
            pltpu.make_async_copy(psi_cond_ref.at[cond_ref[p]], cond_buf.at[spot], sems.at[1, p]),
        )

    @pl.loop(0, pairs)
    def _(p):
        for copy in copies(p):
            copy.start()

    @pl.loop(0, pairs)
    def _(p):
        for copy in copies(p):
            copy.wait()

    def transform(u):
        y, xi = u // xi_count, u % xi_count
        parts = []
        for xo in range(xo_count):
            spot = pl.ds((xo * xi_count + xi) * yb + y, pairs, stride=rows + 8)
            parts.append(val_buf[spot, :] * cond_buf[spot, :])
        high, low = split(jnp.concatenate(parts, axis=0))
        both = jnp.concatenate([high, low], axis=1)
        z = lax.dot_general(wide_ref[...], both, NT, preferred_element_type=F32)
        return z[: 2 * ROW_PAD] + z[2 * ROW_PAD :]

    @pl.loop(0, 16)
    def _(i):
        results = [transform(i * 4 + k) for k in range(4)]
        for k, z in enumerate(results):
            for t in range(width // LANES):
                lanes = slice(t * LANES, (t + 1) * LANES)
                z_buf[t, pl.ds(i * 4 + k, ROW_PAD, stride=Z_STRIDE), :] = z[:ROW_PAD, lanes]
                z_buf[t, pl.ds(64 + i * 4 + k, ROW_PAD, stride=Z_STRIDE), :] = z[ROW_PAD:, lanes]

    @pl.loop(0, half)
    def _(kz):
        for t in range(width // LANES):
            high, low = split(z_buf[t, pl.ds(pl.multiple_of(kz * Z_STRIDE, 8), LANES), :])
            lanes = slice(t * LANES, (t + 1) * LANES)
            zz_buf[pl.ds(pl.multiple_of(kz * 256, 256), LANES), lanes] = high
            zz_buf[pl.ds(pl.multiple_of(kz * 256 + LANES, LANES), LANES), lanes] = low

    lane = lax.broadcasted_iota(jnp.int32, (LANES, LANES), 1)
    u_lane = lane % 64
    y_lane, xi_lane = (u_lane // xi_count).astype(F32), (u_lane % xi_count).astype(F32)
    x_corner = (lax.axis_index("row") * xb).astype(F32)
    y_corner = (lax.axis_index("col") * yb).astype(F32)
    is_im = lane >= 64
    table = jnp.broadcast_to(cos_ref[...], (LANES, LANES))
    quarter = grid // 4

    def cosine(steps):
        return jnp.take_along_axis(table, steps & (grid - 1), axis=1, mode="promise_in_bounds")

    def elements(j, bins):
        def column(low, high):
            row = ordered_ref[pl.ds(low * chunks + j, 1), :] + LANES * ordered_ref[pl.ds(high * chunks + j, 1), :]
            return jnp.broadcast_to(row, (LANES, LANES)).T

        plane = column(0, 1).astype(jnp.int32)
        kx = (plane & (LANES - 1)).astype(F32)
        ky = (plane // LANES).astype(F32)
        folded = column(2, 3).astype(jnp.int32)
        fold = folded & (LANES - 1)
        steps = (ky * y_lane + kx * xi_lane).astype(jnp.int32)
        top = cosine(steps - jnp.where(is_im, quarter, 0))
        bottom = cosine(steps + jnp.where(is_im, 0, quarter))
        left, right = [], []
        for f in bins:
            mine = fold == f
            high, low = split(jnp.concatenate([jnp.where(mine, top, 0.0), jnp.where(mine, bottom, 0.0)], axis=0))
            base = pl.multiple_of(jnp.minimum(f, half - 1) * 256, 256)
            left += [high, high, low]
            right += [zz_buf[pl.ds(base, 256), :], zz_buf[pl.ds(base, LANES), :]]
        result = jnp.dot(
            jnp.concatenate(left, axis=1), jnp.concatenate(right, axis=0), preferred_element_type=F32
        )
        m_re = jnp.zeros((LANES, LANES), F32)
        m_im = jnp.zeros((LANES, LANES), F32)
        for t in range(width // LANES):
            lanes = slice(t * LANES, (t + 1) * LANES)
            x_lane = x_corner + ((t * LANES + lane) // pairs * xi_count).astype(F32)
            steps = (kx * x_lane + ky * y_corner).astype(jnp.int32)
            cos_p, sin_p = cosine(steps), cosine(steps - quarter)
            a_re, a_im = result[:LANES, lanes], result[LANES:, lanes]
            m_re = m_re + a_re * cos_p + a_im * sin_p
            m_im = m_im + a_im * cos_p - a_re * sin_p
        shift = LANES // 2
        while shift >= pairs:
            m_re = m_re + pltpu.roll(m_re, shift, 1)
            m_im = m_im + pltpu.roll(m_im, shift, 1)
            shift //= 2
        m_im = jnp.where(folded < LANES, m_im, -m_im)
        if pairs < LANES:
            return (jnp.where(lane // pairs % 2 == 0, m_re, m_im),)
        return m_re, m_im

    packs = max(1, LANES // (2 * pairs))
    group = chunks // packs

    @pl.loop(0, group // 2)
    def _(i):
        bases = [i, i + group // 2]
        found = [[elements(b + k * group, (first_ref[b + k * group], first_ref[b + k * group] + 1))
                  for k in range(packs)] for b in bases]
        for b, pieces in zip(bases, found):
            spot = pl.ds(pl.multiple_of(b * LANES, LANES), LANES)
            value = list(pieces[0])
            for k in range(1, packs):
                value[0] = jnp.where(lane // (2 * pairs) == k, pieces[k][0], value[0])
            for t, piece in enumerate(value):
                out_ref[spot, t * LANES : (t + 1) * LANES] = piece

    @pl.loop(0, chunks)
    def _(j):
        @pl.loop(first_ref[j] + 2, last_ref[j] + 1)
        def _(f):
            spot = pl.ds(pl.multiple_of(j % group * LANES, LANES), LANES)
            for t, piece in enumerate(elements(j, (f,))):
                if packs > 1:
                    piece = jnp.where(lane // (2 * pairs) == j // group, piece, 0.0)
                lanes = slice(t * LANES, (t + 1) * LANES)
                out_ref[spot, lanes] = out_ref[spot, lanes] + piece


def sum_plan(rows, mesh_rows, mesh_cols):
    col_groups = [("col", 2**b, 2) for b in range(mesh_cols.bit_length() - 1)]
    row_groups = [("row", 1, mesh_rows)]
    orders = (
        col_groups + row_groups,
        col_groups[:1] + col_groups[:0:-1] + row_groups,
        col_groups[:1] + row_groups + col_groups[1:],
    )
    unit = 8 * mesh_rows * mesh_cols
    units = rows // unit
    first = -(-units * 3 // 8)
    counts = (first, first, units - 2 * first)
    parts, base = [], 0
    halves = [(o, c - c // 2) for o, c in zip(orders, counts)] + [(o, c // 2) for o, c in zip(orders, counts)]
    for order, count in halves:
        if count:
            parts.append((base, count * unit, count, order))
            base += count * unit
    return parts


def all_sum_kernel(parts, in_ref, out_ref, data, land, send_sems, recv_sems):
    groups = parts[0][3]
    steps = len(groups)

    def place_in(group):
        axis, stride, size = group
        return lax.axis_index(axis) // stride % size

    def peer(group, hop):
        axis, stride, size = group
        mine = place_in(group)
        other = (mine + hop) % size
        return other, {axis: lax.axis_index(axis) + (other - mine) * stride}

    barrier = pltpu.get_barrier_semaphore()
    for group in groups:
        for hop in range(1, group[2]):
            pl.semaphore_signal(
                barrier, inc=1, device_id=peer(group, hop)[1], device_id_type=pl.DeviceIdType.MESH
            )
    pl.semaphore_wait(barrier, sum(group[2] - 1 for group in groups))

    layout = []
    for base, rows, _, order in parts:
        here, size, spots, lands = base, rows, [], base
        for group in order:
            size //= group[2]
            spots.append((here, size, lands))
            lands += size * (group[2] - 1)
            here = pl.multiple_of(here + place_in(group) * size, 8)
        layout.append(spots)

    def copies_of(k, step):
        back = step if step < steps else 2 * steps - 1 - step
        here, size, lands = layout[k][back]
        group = parts[k][3][back]
        found = []
        for hop in range(1, group[2]):
            other, device = peer(group, hop)
            if step < steps:
                away = pl.multiple_of(here + other * size, 8)
                source = (in_ref if step == 0 else data).at[pl.ds(away, size)]
                target = land.at[pl.ds(lands + (hop - 1) * size, size)]
            else:
                keep = pl.multiple_of(here + place_in(group) * size, 8)
                source = target = out_ref.at[pl.ds(keep, size)]
            found.append(
                pltpu.make_async_remote_copy(
                    src_ref=source,
                    dst_ref=target,
                    send_sem=send_sems.at[k, step, hop - 1],
                    recv_sem=recv_sems.at[k, step, hop - 1],
                    device_id=device,
                    device_id_type=pl.DeviceIdType.MESH,
                )
            )
        return found

    def add(k, step):
        here, size, lands = layout[k][step]
        group = parts[k][3][step]
        keep = here + place_in(group) * size
        source = in_ref if step == 0 else data
        target = out_ref if step == steps - 1 else data
        piece = min(size, 32 * parts[k][2])

        @pl.loop(0, size // piece)
        def _(i):
            spot = pl.ds(pl.multiple_of(keep + i * piece, 8), piece)
            value = source[spot, :]
            for hop in range(1, group[2]):
                start = lands + (hop - 1) * size + i * piece
                value = value + land[pl.ds(pl.multiple_of(start, 8), piece), :]
            target[spot, :] = value

    for k in range(len(parts)):
        for copy in copies_of(k, 0):
            copy.start()
    for step in range(2 * steps):
        for k in range(len(parts)):
            for copy in copies_of(k, step):
                copy.wait_recv()
            if step < steps:
                add(k, step)
            if step < 2 * steps - 1:
                for copy in copies_of(k, step + 1):
                    copy.start()
    for step in range(2 * steps):
        for k in range(len(parts)):
            for copy in copies_of(k, step):
                copy.wait_send()


def all_sum(value, mesh_rows, mesh_cols):
    parts = sum_plan(value.shape[0], mesh_rows, mesh_cols)
    slots = (len(parts), 2 * len(parts[0][3]), max(group[2] for group in parts[0][3]) - 1)
    vmem_spec = pl.BlockSpec(memory_space=pltpu.VMEM)
    return pl.pallas_call(
        functools.partial(all_sum_kernel, parts),
        out_shape=jax.ShapeDtypeStruct(value.shape, F32),
        in_specs=[vmem_spec],
        out_specs=vmem_spec,
        scratch_shapes=[
            pltpu.VMEM(value.shape, F32),
            pltpu.VMEM(value.shape, F32),
            pltpu.SemaphoreType.DMA(slots),
            pltpu.SemaphoreType.DMA(slots),
        ],
        compiler_params=pltpu.CompilerParams(
            collective_id=0, has_side_effects=True, vmem_limit_bytes=VMEM_BYTES
        ),
        name="all_sum",
    )(value)


def update_kernel(
    dims, place, val_ref, cond_ref, eps_val_ref, eps_cond_ref, total_ref, chi_ref, out_ref,
    m_ref, row_buf, col_buf, right_buf, chi_buf, sems,
):
    pairs, step_rows, cols, wide = dims
    steps = chi_ref.shape[1] // step_rows

    def arrival(step):
        spot = pl.ds(pl.multiple_of(step * step_rows, step_rows), step_rows)
        return pltpu.make_async_copy(chi_ref.at[:, spot], chi_buf.at[:, spot], sems.at[0, step])

    def departure(step):
        spot = pl.ds(pl.multiple_of(step * step_rows, step_rows), step_rows)
        return pltpu.make_async_copy(chi_buf.at[:, spot], out_ref.at[:, spot], sems.at[1, step])

    @pl.loop(0, steps)
    def _(step):
        arrival(step).start()

    def gather(base, buf, count):
        @pl.loop(0, count // 16)
        def _(i):
            found = [m_ref[pl.ds(place[base + i * 16 + k], 1), :] for k in range(16)]
            for half in range(2):
                spot = pl.ds(pl.multiple_of(i * 16 + half * 8, 8), 8)
                buf[spot, :] = jnp.concatenate(found[half * 8 : half * 8 + 8], axis=0)

    def join(value):
        high, low = split(value)
        if 2 * pairs < LANES:
            lane = lax.broadcasted_iota(jnp.int32, value.shape, 1)
            keep = lane < 2 * pairs
            high32, low32 = high.astype(F32), low.astype(F32)
            return jnp.concatenate(
                [jnp.where(keep, high32, low32).astype(BF16), jnp.where(keep, high32, 0.0).astype(BF16)], axis=1
            )
        return jnp.concatenate([high, low, high], axis=1)

    def join_right(value):
        high, low = split(value)
        if 2 * pairs < LANES:
            keep = lax.broadcasted_iota(jnp.int32, value.shape, 0) < 2 * pairs
            return jnp.concatenate([high, jnp.where(keep, low.astype(F32), 0.0).astype(BF16)], axis=0)
        return jnp.concatenate([high, high, low], axis=0)

    pair_lane = lax.broadcasted_iota(jnp.int32, (8, wide), 1) % pairs

    def set_gap(p, gaps):
        return jnp.where(pair_lane == p, eps_cond_ref[cond_ref[p]] - eps_val_ref[val_ref[p]], gaps)

    gaps = lax.fori_loop(0, pairs, set_gap, jnp.ones((8, wide), F32))
    weight = (-6.0 / (math.sqrt(pairs) * gaps))[:1]
    packed = total_ref.shape[0]
    piece = 64

    @pl.loop(0, packed // piece)
    def _(i):
        value = total_ref[pl.ds(pl.multiple_of(i * piece, piece), piece), :]
        lane = lax.broadcasted_iota(jnp.int32, value.shape, 1)
        for q in range(m_ref.shape[0] // packed):
            part = value
            if 2 * pairs < wide:
                part = jnp.where(lane // (2 * pairs) == q, value, 0.0)
                shift = 2 * pairs
                while shift < wide:
                    part = part + pltpu.roll(part, shift, 1)
                    shift *= 2
            m_ref[pl.ds(pl.multiple_of(q * packed + i * piece, piece), piece), :] = part

    gather(lax.axis_index("col") * cols, col_buf, cols)
    right_buf[...] = join_right(col_buf[...].T)

    @pl.loop(0, steps)
    def _(step):
        gather((lax.axis_index("row") * steps + step) * step_rows, row_buf, step_rows)
        left = row_buf[...] * weight
        lane = lax.broadcasted_iota(jnp.int32, left.shape, 1)
        turned = pltpu.roll(left, wide - pairs, 1)
        turned = jnp.where(lane // pairs % 2 == 0, turned, -turned)
        arrival(step).wait()
        spot = pl.ds(pl.multiple_of(step * step_rows, step_rows), step_rows)
        for part, factor in enumerate((left, turned)):
            change = jnp.dot(join(factor), right_buf[...], preferred_element_type=F32)
            chi_buf[part, spot, :] = chi_buf[part, spot, :] + change
        departure(step).start()

    @pl.loop(0, steps)
    def _(step):
        departure(step).wait()


def on_device(psi_val, psi_cond, eps_val, eps_cond, val_index, cond_index, gmap, chi0_in):
    pairs = val_index.shape[0]
    bands_v, xb, yb, grid = psi_val.shape
    bands_c = psi_cond.shape[0]
    points = gmap.shape[0]
    chunks = points // LANES
    place, ordered = sort_points(gmap, grid)
    fold = ordered[2 * chunks : 3 * chunks].astype(jnp.int32)
    z_wide = z_tables(grid)
    cos_row = jnp.asarray(np.cos(np.arange(grid) * (2.0 * math.pi / grid))[None, :], F32)
    wide = max(LANES, 2 * pairs)
    xi_count = 64 // yb
    width = xb // xi_count * pairs
    rows = xb * yb
    any_spec = pl.BlockSpec(memory_space=pl.ANY)
    vmem_spec = pl.BlockSpec(memory_space=pltpu.VMEM)
    partial = pl.pallas_call(
        functools.partial(partial_kernel, (pairs, xb, yb, grid, chunks)),
        out_shape=jax.ShapeDtypeStruct((points * 2 * pairs // wide, wide), F32),
        grid_spec=pltpu.PrefetchScalarGridSpec(
            num_scalar_prefetch=4,
            grid=(),
            in_specs=[vmem_spec] * 3 + [any_spec] * 2,
            out_specs=vmem_spec,
            scratch_shapes=[
                pltpu.VMEM((pairs * (rows + 8), grid), F32),
                pltpu.VMEM((pairs * (rows + 8), grid), F32),
                pltpu.VMEM((width // LANES, ROW_PAD * Z_STRIDE, LANES), F32),
                pltpu.VMEM(((grid // 2 + 1) * 256, width), BF16),
                pltpu.SemaphoreType.DMA((2, pairs)),
            ],
        ),
        compiler_params=pltpu.CompilerParams(vmem_limit_bytes=VMEM_BYTES),
        name="partial_elements",
    )(
        val_index, cond_index, fold[:, 0], fold[:, LANES - 1],
        ordered, z_wide, cos_row,
        psi_val.reshape(bands_v, rows, grid), psi_cond.reshape(bands_c, rows, grid),
    )
    total = all_sum(partial, lax.axis_size("row"), lax.axis_size("col"))

    _, row_span, col_span = chi0_in.shape
    step_rows = 256
    k_width = 256 if 2 * pairs < LANES else 3 * wide
    return pl.pallas_call(
        functools.partial(update_kernel, (pairs, step_rows, col_span, wide)),
        out_shape=jax.ShapeDtypeStruct(chi0_in.shape, F32),
        grid_spec=pltpu.PrefetchScalarGridSpec(
            num_scalar_prefetch=5,
            grid=(),
            in_specs=[vmem_spec, any_spec],
            out_specs=any_spec,
            scratch_shapes=[
                pltpu.VMEM((points, wide), F32),
                pltpu.VMEM((step_rows, wide), F32),
                pltpu.VMEM((col_span, wide), F32),
                pltpu.VMEM((k_width, col_span), BF16),
                pltpu.VMEM(chi0_in.shape, F32),
                pltpu.SemaphoreType.DMA((2, row_span // step_rows)),
            ],
        ),
        compiler_params=pltpu.CompilerParams(vmem_limit_bytes=VMEM_BYTES),
        name="chi_update",
    )(place, val_index, cond_index, eps_val, eps_cond, total, chi0_in)


def solution(mesh):
    return jax.shard_map(
        on_device,
        mesh=mesh,
        in_specs=(
            P(None, "row", "col", None),
            P(None, "row", "col", None),
            P(),
            P(),
            P(),
            P(),
            P(),
            P(None, "row", "col"),
        ),
        out_specs=P(None, "row", "col"),
        check_vma=False,
    )
```

```python
import functools
import math

import jax
import jax.numpy as jnp
import ml_dtypes
import numpy as np
from jax import lax
from jax.experimental import pallas as pl
from jax.experimental.pallas import tpu as pltpu
from jax.sharding import PartitionSpec as P

F32 = jnp.float32
BF16 = jnp.bfloat16
LANES = 128
ROW_PAD = 72
Z_STRIDE = LANES + 8
VMEM_BYTES = 60 * 1024 * 1024
NT = (((1,), (1,)), ((), ()))


def split(value):
    high = value.astype(BF16)
    return high, (value - high.astype(F32)).astype(BF16)


def z_tables(grid):
    half = grid // 2 + 1
    freq = np.arange(half)[:, None] * np.arange(grid)[None, :] % grid
    angle = freq * (2.0 * math.pi / grid)
    scale = 1.0 / math.sqrt(grid**3)
    table = np.zeros((2 * ROW_PAD, grid), np.float32)
    table[:half] = np.cos(angle) * scale
    table[ROW_PAD : ROW_PAD + half] = -np.sin(angle) * scale
    high = table.astype(ml_dtypes.bfloat16)
    low = (table - high.astype(np.float32)).astype(ml_dtypes.bfloat16)
    top = np.concatenate([high, high], axis=1)
    return jnp.asarray(np.concatenate([top, np.concatenate([low, np.zeros_like(low)], axis=1)], axis=0))


def sort_points(gmap, grid):
    count = gmap.shape[0]
    blocks = count // LANES
    kx = gmap // (grid * grid)
    ky = gmap // grid % grid
    kz = gmap % grid
    flip = kz > grid // 2
    fold = jnp.where(flip, grid - kz, kz)
    kx = jnp.where(flip, (grid - kx) % grid, kx)
    ky = jnp.where(flip, (grid - ky) % grid, ky)
    sign = flip.astype(F32)
    bins = jnp.arange(LANES, dtype=jnp.int32)
    hot = (fold.reshape(blocks, LANES)[:, :, None] == bins).astype(BF16)
    before = (bins[:, None] > bins[None, :]).astype(BF16)
    within = jnp.einsum("ab,jbk->jak", before, hot, preferred_element_type=F32)
    totals = jnp.sum(hot.astype(F32), axis=1).astype(BF16)
    offset = jnp.dot(before[:blocks, :blocks], totals, preferred_element_type=F32)
    start = jnp.sum(jnp.dot(totals, before.T, preferred_element_type=F32), axis=0)
    place = jnp.sum(hot.astype(F32) * (within + offset[:, None, :] + start), axis=2)
    place = place.reshape(-1).astype(jnp.int32)
    major = (place[:, None] // LANES == jnp.arange(blocks, dtype=jnp.int32)).astype(F32)
    minor = (place[:, None] % LANES == bins).astype(BF16)
    values = jnp.stack([kx.astype(F32), ky.astype(F32), fold.astype(F32), sign], axis=1)
    spread = (values[:, :, None] * major[:, None, :]).reshape(count, 4 * blocks).astype(BF16)
    ordered = lax.dot_general(spread, minor, (((0,), (0,)), ((), ())), preferred_element_type=F32)
    return place, ordered


def partial_kernel(
    dims, val_ref, cond_ref, first_ref, last_ref,
    ordered_ref, wide_ref, cos_ref, psi_val_ref, psi_cond_ref,
    out_ref, val_buf, cond_buf, z_buf, zz_buf, sems,
):
    pairs, xb, yb, grid, chunks = dims
    rows = xb * yb
    xi_count = 64 // yb
    xo_count = xb // xi_count
    width = xo_count * pairs
    half = grid // 2 + 1

    def copies(p, part):
        here = pl.ds(part * (rows // 2), rows // 2)
        spot = pl.ds(pl.multiple_of(p * (rows + 8) + part * (rows // 2), 8), rows // 2)
        return (
            pltpu.make_async_copy(psi_val_ref.at[val_ref[p], here], val_buf.at[spot], sems.at[0, part, p]),
            pltpu.make_async_copy(psi_cond_ref.at[cond_ref[p], here], cond_buf.at[spot], sems.at[1, part, p]),
        )

    def transform(y, xi):
        parts = []
        for xo in range(xo_count):
            spot = pl.ds((xi * xo_count + xo) * yb + y, pairs, stride=rows + 8)
            parts.append(val_buf[spot, :] * cond_buf[spot, :])
        high, low = split(jnp.concatenate(parts, axis=0))
        both = jnp.concatenate([high, low], axis=1)
        z = lax.dot_general(wide_ref[...], both, NT, preferred_element_type=F32)
        return z[: 2 * ROW_PAD] + z[2 * ROW_PAD :]

    for part in range(2):

        @pl.loop(0, pairs)
        def _(p):
            for copy in copies(p, part):
                copy.start()

    for part in range(2):

        @pl.loop(0, pairs)
        def _(p):
            for copy in copies(p, part):
                copy.wait()

        @pl.loop(0, 8)
        def _(i):
            spots = [((i * 4 + k) % yb, part * (xi_count // 2) + (i * 4 + k) // yb) for k in range(4)]
            results = [transform(y, xi) for y, xi in spots]
            for (y, xi), z in zip(spots, results):
                u = y * xi_count + xi
                for t in range(width // LANES):
                    lanes = slice(t * LANES, (t + 1) * LANES)
                    z_buf[t, pl.ds(u, ROW_PAD, stride=Z_STRIDE), :] = z[:ROW_PAD, lanes]
                    z_buf[t, pl.ds(64 + u, ROW_PAD, stride=Z_STRIDE), :] = z[ROW_PAD:, lanes]

    @pl.loop(0, half)
    def _(kz):
        for t in range(width // LANES):
            high, low = split(z_buf[t, pl.ds(pl.multiple_of(kz * Z_STRIDE, 8), LANES), :])
            lanes = slice(t * LANES, (t + 1) * LANES)
            zz_buf[pl.ds(pl.multiple_of(kz * 256, 256), LANES), lanes] = high
            zz_buf[pl.ds(pl.multiple_of(kz * 256 + LANES, LANES), LANES), lanes] = low

    lane = lax.broadcasted_iota(jnp.int32, (LANES, LANES), 1)
    u_lane = lane % 64
    y_lane, xi_lane = (u_lane // xi_count).astype(F32), (u_lane % xi_count * xo_count).astype(F32)
    x_corner = (lax.axis_index("row") * xb).astype(F32)
    y_corner = (lax.axis_index("col") * yb).astype(F32)
    is_im = lane >= 64
    table = jnp.broadcast_to(cos_ref[...], (LANES, LANES))
    quarter = grid // 4

    def cosine(steps):
        return jnp.take_along_axis(table, steps & (grid - 1), axis=1, mode="promise_in_bounds")

    def elements(j, bins):
        def column(low, high):
            row = ordered_ref[pl.ds(low * chunks + j, 1), :] + LANES * ordered_ref[pl.ds(high * chunks + j, 1), :]
            return jnp.broadcast_to(row, (LANES, LANES)).T

        plane = column(0, 1).astype(jnp.int32)
        kx = (plane & (LANES - 1)).astype(F32)
        ky = (plane // LANES).astype(F32)
        folded = column(2, 3).astype(jnp.int32)
        fold = folded & (LANES - 1)
        steps = (ky * y_lane + kx * xi_lane).astype(jnp.int32)
        top = cosine(steps - jnp.where(is_im, quarter, 0))
        bottom = cosine(steps + jnp.where(is_im, 0, quarter))
        left, right = [], []
        for f in bins:
            mine = fold == f
            high, low = split(jnp.concatenate([jnp.where(mine, top, 0.0), jnp.where(mine, bottom, 0.0)], axis=0))
            base = pl.multiple_of(jnp.minimum(f, half - 1) * 256, 256)
            left += [high, high, low]
            right += [zz_buf[pl.ds(base, 256), :], zz_buf[pl.ds(base, LANES), :]]
        result = jnp.dot(
            jnp.concatenate(left, axis=1), jnp.concatenate(right, axis=0), preferred_element_type=F32
        )
        m_re = jnp.zeros((LANES, LANES), F32)
        m_im = jnp.zeros((LANES, LANES), F32)
        for t in range(width // LANES):
            lanes = slice(t * LANES, (t + 1) * LANES)
            x_lane = x_corner + ((t * LANES + lane) // pairs).astype(F32)
            steps = (kx * x_lane + ky * y_corner).astype(jnp.int32)
            cos_p, sin_p = cosine(steps), cosine(steps - quarter)
            a_re, a_im = result[:LANES, lanes], result[LANES:, lanes]
            m_re = m_re + a_re * cos_p + a_im * sin_p
            m_im = m_im + a_im * cos_p - a_re * sin_p
        shift = LANES // 2
        while shift >= pairs:
            m_re = m_re + pltpu.roll(m_re, shift, 1)
            m_im = m_im + pltpu.roll(m_im, shift, 1)
            shift //= 2
        m_im = jnp.where(folded < LANES, m_im, -m_im)
        if pairs < LANES:
            return (jnp.where(lane // pairs % 2 == 0, m_re, m_im),)
        return m_re, m_im

    packs = max(1, LANES // (2 * pairs))
    group = chunks // packs

    @pl.loop(0, group // 2)
    def _(i):
        bases = [i, i + group // 2]
        found = [[elements(b + k * group, (first_ref[b + k * group], first_ref[b + k * group] + 1))
                  for k in range(packs)] for b in bases]
        for b, pieces in zip(bases, found):
            spot = pl.ds(pl.multiple_of(b * LANES, LANES), LANES)
            value = list(pieces[0])
            for k in range(1, packs):
                value[0] = jnp.where(lane // (2 * pairs) == k, pieces[k][0], value[0])
            for t, piece in enumerate(value):
                out_ref[spot, t * LANES : (t + 1) * LANES] = piece

    @pl.loop(0, chunks)
    def _(j):
        @pl.loop(first_ref[j] + 2, last_ref[j] + 1)
        def _(f):
            spot = pl.ds(pl.multiple_of(j % group * LANES, LANES), LANES)
            for t, piece in enumerate(elements(j, (f,))):
                if packs > 1:
                    piece = jnp.where(lane // (2 * pairs) == j // group, piece, 0.0)
                lanes = slice(t * LANES, (t + 1) * LANES)
                out_ref[spot, lanes] = out_ref[spot, lanes] + piece


def sum_plan(rows, mesh_rows, mesh_cols):
    col_groups = [("col", 2**b, 2) for b in range(mesh_cols.bit_length() - 1)]
    row_groups = [("row", 1, mesh_rows)]
    orders = (
        col_groups + row_groups,
        col_groups[:1] + col_groups[:0:-1] + row_groups,
        col_groups[:1] + row_groups + col_groups[1:],
    )
    unit = 8 * mesh_rows * mesh_cols
    units = rows // unit
    first = -(-units * 3 // 8)
    counts = (first, first, units - 2 * first)
    parts, base = [], 0
    halves = [(o, c - c // 2) for o, c in zip(orders, counts)] + [(o, c // 2) for o, c in zip(orders, counts)]
    for order, count in halves:
        if count:
            parts.append((base, count * unit, count, order))
            base += count * unit
    return parts


def all_sum_kernel(parts, in_ref, out_ref, data, land, send_sems, recv_sems):
    groups = parts[0][3]
    steps = len(groups)

    def place_in(group):
        axis, stride, size = group
        return lax.axis_index(axis) // stride % size

    def peer(group, hop):
        axis, stride, size = group
        mine = place_in(group)
        other = (mine + hop) % size
        return other, {axis: lax.axis_index(axis) + (other - mine) * stride}

    barrier = pltpu.get_barrier_semaphore()
    for group in groups:
        for hop in range(1, group[2]):
            pl.semaphore_signal(
                barrier, inc=1, device_id=peer(group, hop)[1], device_id_type=pl.DeviceIdType.MESH
            )
    pl.semaphore_wait(barrier, sum(group[2] - 1 for group in groups))

    layout = []
    for base, rows, _, order in parts:
        here, size, spots, lands = base, rows, [], base
        for group in order:
            size //= group[2]
            spots.append((here, size, lands))
            lands += size * (group[2] - 1)
            here = pl.multiple_of(here + place_in(group) * size, 8)
        layout.append(spots)

    def copies_of(k, step):
        back = step if step < steps else 2 * steps - 1 - step
        here, size, lands = layout[k][back]
        group = parts[k][3][back]
        found = []
        for hop in range(1, group[2]):
            other, device = peer(group, hop)
            if step < steps:
                away = pl.multiple_of(here + other * size, 8)
                source = (in_ref if step == 0 else data).at[pl.ds(away, size)]
                target = land.at[pl.ds(lands + (hop - 1) * size, size)]
            else:
                keep = pl.multiple_of(here + place_in(group) * size, 8)
                source = target = out_ref.at[pl.ds(keep, size)]
            found.append(
                pltpu.make_async_remote_copy(
                    src_ref=source,
                    dst_ref=target,
                    send_sem=send_sems.at[k, step, hop - 1],
                    recv_sem=recv_sems.at[k, step, hop - 1],
                    device_id=device,
                    device_id_type=pl.DeviceIdType.MESH,
                )
            )
        return found

    def add(k, step):
        here, size, lands = layout[k][step]
        group = parts[k][3][step]
        keep = here + place_in(group) * size
        source = in_ref if step == 0 else data
        target = out_ref if step == steps - 1 else data
        piece = min(size, 32 * parts[k][2])

        @pl.loop(0, size // piece)
        def _(i):
            spot = pl.ds(pl.multiple_of(keep + i * piece, 8), piece)
            value = source[spot, :]
            for hop in range(1, group[2]):
                start = lands + (hop - 1) * size + i * piece
                value = value + land[pl.ds(pl.multiple_of(start, 8), piece), :]
            target[spot, :] = value

    for k in range(len(parts)):
        for copy in copies_of(k, 0):
            copy.start()
    for step in range(2 * steps):
        for k in range(len(parts)):
            for copy in copies_of(k, step):
                copy.wait_recv()
            if step < steps:
                add(k, step)
            if step < 2 * steps - 1:
                for copy in copies_of(k, step + 1):
                    copy.start()
    for step in range(2 * steps):
        for k in range(len(parts)):
            for copy in copies_of(k, step):
                copy.wait_send()


def all_sum(value, mesh_rows, mesh_cols):
    parts = sum_plan(value.shape[0], mesh_rows, mesh_cols)
    slots = (len(parts), 2 * len(parts[0][3]), max(group[2] for group in parts[0][3]) - 1)
    vmem_spec = pl.BlockSpec(memory_space=pltpu.VMEM)
    return pl.pallas_call(
        functools.partial(all_sum_kernel, parts),
        out_shape=jax.ShapeDtypeStruct(value.shape, F32),
        in_specs=[vmem_spec],
        out_specs=vmem_spec,
        scratch_shapes=[
            pltpu.VMEM(value.shape, F32),
            pltpu.VMEM(value.shape, F32),
            pltpu.SemaphoreType.DMA(slots),
            pltpu.SemaphoreType.DMA(slots),
        ],
        compiler_params=pltpu.CompilerParams(
            collective_id=0, has_side_effects=True, vmem_limit_bytes=VMEM_BYTES
        ),
        name="all_sum",
    )(value)


def update_kernel(
    dims, place, val_ref, cond_ref, eps_val_ref, eps_cond_ref, total_ref, chi_ref, out_ref,
    m_ref, row_buf, col_buf, right_buf, chi_buf, sems,
):
    pairs, step_rows, cols, wide = dims
    steps = chi_ref.shape[1] // step_rows

    def arrival(step):
        spot = pl.ds(pl.multiple_of(step * step_rows, step_rows), step_rows)
        return pltpu.make_async_copy(chi_ref.at[:, spot], chi_buf.at[:, spot], sems.at[0, step])

    def departure(step):
        spot = pl.ds(pl.multiple_of(step * step_rows, step_rows), step_rows)
        return pltpu.make_async_copy(chi_buf.at[:, spot], out_ref.at[:, spot], sems.at[1, step])

    @pl.loop(0, steps)
    def _(step):
        arrival(step).start()

    def gather(base, buf, count):
        @pl.loop(0, count // 64)
        def _(i):
            found = [m_ref[pl.ds(place[base + i * 64 + k], 1), :] for k in range(64)]
            for tile in range(8):
                spot = pl.ds(pl.multiple_of(i * 64 + tile * 8, 8), 8)
                buf[spot, :] = jnp.concatenate(found[tile * 8 : tile * 8 + 8], axis=0)

    def join(value):
        high, low = split(value)
        if 2 * pairs < LANES:
            lane = lax.broadcasted_iota(jnp.int32, value.shape, 1)
            keep = lane < 2 * pairs
            high32, low32 = high.astype(F32), low.astype(F32)
            return jnp.concatenate(
                [jnp.where(keep, high32, low32).astype(BF16), jnp.where(keep, high32, 0.0).astype(BF16)], axis=1
            )
        return jnp.concatenate([high, low, high], axis=1)

    def join_right(value):
        high, low = split(value)
        if 2 * pairs < LANES:
            keep = lax.broadcasted_iota(jnp.int32, value.shape, 0) < 2 * pairs
            return jnp.concatenate([high, jnp.where(keep, low.astype(F32), 0.0).astype(BF16)], axis=0)
        return jnp.concatenate([high, high, low], axis=0)

    pair_lane = lax.broadcasted_iota(jnp.int32, (8, wide), 1) % pairs

    def set_gap(p, gaps):
        return jnp.where(pair_lane == p, eps_cond_ref[cond_ref[p]] - eps_val_ref[val_ref[p]], gaps)

    gaps = lax.fori_loop(0, pairs, set_gap, jnp.ones((8, wide), F32))
    weight = (-6.0 / (math.sqrt(pairs) * gaps))[:1]
    packed = total_ref.shape[0]
    piece = 64

    @pl.loop(0, packed // piece)
    def _(i):
        value = total_ref[pl.ds(pl.multiple_of(i * piece, piece), piece), :]
        lane = lax.broadcasted_iota(jnp.int32, value.shape, 1)
        for q in range(m_ref.shape[0] // packed):
            part = value
            if 2 * pairs < wide:
                part = jnp.where(lane // (2 * pairs) == q, value, 0.0)
                shift = 2 * pairs
                while shift < wide:
                    part = part + pltpu.roll(part, shift, 1)
                    shift *= 2
            m_ref[pl.ds(pl.multiple_of(q * packed + i * piece, piece), piece), :] = part

    gather(lax.axis_index("col") * cols, col_buf, cols)
    right_buf[...] = join_right(col_buf[...].T)

    @pl.loop(0, steps)
    def _(step):
        gather((lax.axis_index("row") * steps + step) * step_rows, row_buf, step_rows)
        left = row_buf[...] * weight
        lane = lax.broadcasted_iota(jnp.int32, left.shape, 1)
        turned = pltpu.roll(left, wide - pairs, 1)
        turned = jnp.where(lane // pairs % 2 == 0, turned, -turned)
        arrival(step).wait()
        spot = pl.ds(pl.multiple_of(step * step_rows, step_rows), step_rows)
        for part, factor in enumerate((left, turned)):
            change = jnp.dot(join(factor), right_buf[...], preferred_element_type=F32)
            chi_buf[part, spot, :] = chi_buf[part, spot, :] + change
        departure(step).start()

    @pl.loop(0, steps)
    def _(step):
        departure(step).wait()


def on_device(psi_val, psi_cond, eps_val, eps_cond, val_index, cond_index, gmap, chi0_in):
    pairs = val_index.shape[0]
    bands_v, xb, yb, grid = psi_val.shape
    bands_c = psi_cond.shape[0]
    points = gmap.shape[0]
    chunks = points // LANES
    place, ordered = sort_points(gmap, grid)
    fold = ordered[2 * chunks : 3 * chunks].astype(jnp.int32)
    z_wide = z_tables(grid)
    cos_row = jnp.asarray(np.cos(np.arange(grid) * (2.0 * math.pi / grid))[None, :], F32)
    wide = max(LANES, 2 * pairs)
    xi_count = 64 // yb
    width = xb // xi_count * pairs
    rows = xb * yb
    any_spec = pl.BlockSpec(memory_space=pl.ANY)
    vmem_spec = pl.BlockSpec(memory_space=pltpu.VMEM)
    partial = pl.pallas_call(
        functools.partial(partial_kernel, (pairs, xb, yb, grid, chunks)),
        out_shape=jax.ShapeDtypeStruct((points * 2 * pairs // wide, wide), F32),
        grid_spec=pltpu.PrefetchScalarGridSpec(
            num_scalar_prefetch=4,
            grid=(),
            in_specs=[vmem_spec] * 3 + [any_spec] * 2,
            out_specs=vmem_spec,
            scratch_shapes=[
                pltpu.VMEM(((pairs + 1) * (rows + 8), grid), F32),
                pltpu.VMEM(((pairs + 1) * (rows + 8), grid), F32),
                pltpu.VMEM((width // LANES, (ROW_PAD + 1) * Z_STRIDE, LANES), F32),
                pltpu.VMEM(((grid // 2 + 1) * 256, width), BF16),
                pltpu.SemaphoreType.DMA((2, 2, pairs)),
            ],
        ),
        compiler_params=pltpu.CompilerParams(vmem_limit_bytes=VMEM_BYTES),
        name="partial_elements",
    )(
        val_index, cond_index, fold[:, 0], fold[:, LANES - 1],
        ordered, z_wide, cos_row,
        psi_val.reshape(bands_v, rows, grid), psi_cond.reshape(bands_c, rows, grid),
    )
    total = all_sum(partial, lax.axis_size("row"), lax.axis_size("col"))

    _, row_span, col_span = chi0_in.shape
    step_rows = 256
    k_width = 256 if 2 * pairs < LANES else 3 * wide
    return pl.pallas_call(
        functools.partial(update_kernel, (pairs, step_rows, col_span, wide)),
        out_shape=jax.ShapeDtypeStruct(chi0_in.shape, F32),
        grid_spec=pltpu.PrefetchScalarGridSpec(
            num_scalar_prefetch=5,
            grid=(),
            in_specs=[vmem_spec, any_spec],
            out_specs=any_spec,
            scratch_shapes=[
                pltpu.VMEM((points, wide), F32),
                pltpu.VMEM((step_rows, wide), F32),
                pltpu.VMEM((col_span, wide), F32),
                pltpu.VMEM((k_width, col_span), BF16),
                pltpu.VMEM(chi0_in.shape, F32),
                pltpu.SemaphoreType.DMA((2, row_span // step_rows)),
            ],
        ),
        compiler_params=pltpu.CompilerParams(vmem_limit_bytes=VMEM_BYTES),
        name="chi_update",
    )(place, val_index, cond_index, eps_val, eps_cond, total, chi0_in)


def solution(mesh):
    return jax.shard_map(
        on_device,
        mesh=mesh,
        in_specs=(
            P(None, "row", "col", None),
            P(None, "row", "col", None),
            P(),
            P(),
            P(),
            P(),
            P(),
            P(None, "row", "col"),
        ),
        out_specs=P(None, "row", "col"),
        check_vma=False,
    )
```
